256 devices in a mesh: row: 8 (over x, core), col: 32 (over z, y).
Axes of the slice: x: 4, y: 4, z: 8, core: 2. Of those that a mesh axis runs over, the one named last changes fastest.
Arguments:
- images: bfloat16 [24576, 768], P(('row', 'col')), may hold values from -16 to 16
- texts: bfloat16 [24576, 768], P(('row', 'col')), may hold values from -16 to 16
- logit_scale: float32 [1], replicated, may hold values from 0.05 to 0.15
Outputs:
- loss: float32 [1], replicated
- grad_images: float32 [24576, 768], P(('row', 'col'))
- grad_texts: float32 [24576, 768], P(('row', 'col'))
The draws below stay inside these ranges and needn't reach their ends.
All inputs are finite; a program needn't handle non-finite values.
Results may differ from the reference program's by a relative error of at most 0.002.
Values may be sent and summed in bfloat16 or wider, within the bound.
A program may use at most 192 MiB of HBM per device.

```python
import math
import jax
import jax.numpy as jnp
from jax import lax

E = 768
PAIRS = 24576


def shared_texts(key):
    return jnp.clip(jax.random.normal(key, (PAIRS, E), jnp.float32), -6.0, 6.0)


def aligned_rows(key):
    sign_key = jax.random.fold_in(key, 11)
    signs = jnp.where(jax.random.bernoulli(sign_key, 0.5, (PAIRS, E)), 1.0, -1.0).astype(jnp.float32)
    index = jnp.arange(PAIRS, dtype=jnp.int32)[:, None]
    group = index % 61
    lead = group == 0
    follow = group == 1
    previous = jnp.roll(signs, 1, axis=0)
    pattern = jnp.where(follow, previous * (1.0 - 1.0 / 300.0), signs)
    level = (index // 61 % 3).astype(jnp.float32)
    amplitude = jnp.sqrt(6000.0 / E) * (1.0 - 0.15 * level)
    return (lead | follow, amplitude * pattern)


def draw_texts(key, part):
    mask, values = aligned_rows(key)
    base = shared_texts(key)
    return jnp.clip(jnp.where(mask, values, base), -16.0, 16.0).astype(jnp.bfloat16)


def draw_images(key, part):
    mask, values = aligned_rows(key)
    key = jax.random.fold_in(key, 5)
    drawn = jnp.clip(jax.random.normal(key, (PAIRS, E), jnp.float32), -6.0, 6.0)
    return jnp.clip(jnp.where(mask, values, drawn), -16.0, 16.0).astype(jnp.bfloat16)


def setup_inputs(seed: int = 0) -> dict:
    key_list = jax.random.split(jax.random.key(seed), 4)
    images = draw_images(jax.random.fold_in(key_list[3], 71), 0)
    texts = draw_texts(jax.random.fold_in(key_list[3], 71), 0)
    logit_scale = jnp.clip(jnp.exp(jax.random.uniform(key_list[2], (1,), jnp.float32, math.log(0.05), math.log(0.15))), 0.05, 0.15)
    return {"images": images, "texts": texts, "logit_scale": logit_scale}


def tile_scores(block, texts, scale):
    return scale * lax.dot_general(block, texts, (((1,), (1,)), ((), ())), preferred_element_type=jnp.float32)


def reference(images, texts, logit_scale):
    scale = logit_scale[0]
    total = images.shape[0]
    width = images.shape[1]
    step_rows = math.gcd(total, 2048)
    count = total // step_rows
    image_blocks = images.reshape(count, step_rows, width)

    def first_pass(carry, block):
        col_max, col_sum = carry
        scores = tile_scores(block, texts, scale)
        row_max = jnp.max(scores, axis=1)
        lse_rows = row_max + jnp.log(jnp.sum(jnp.exp(scores - row_max[:, None]), axis=1))
        new_max = jnp.maximum(col_max, jnp.max(scores, axis=0))
        new_sum = col_sum * jnp.exp(col_max - new_max) + jnp.sum(jnp.exp(scores - new_max[None, :]), axis=0)
        return (new_max, new_sum), lse_rows

    start = (jnp.full((total,), -jnp.inf, jnp.float32), jnp.zeros((total,), jnp.float32))
    (col_max, col_sum), lse_img = lax.scan(first_pass, start, image_blocks)
    lse_txt = col_max + jnp.log(col_sum)
    lse_blocks = lse_img

    def second_pass(acc, inputs):
        block, lse_rows = inputs
        scores = tile_scores(block, texts, scale)
        weights = ((jnp.exp(scores - lse_rows[:, None]) + jnp.exp(scores - lse_txt[None, :])) * (scale * 0.5)).astype(jnp.bfloat16)
        grad_rows = jnp.dot(weights, texts, preferred_element_type=jnp.float32)
        acc = acc + lax.dot_general(weights, block, (((0,), (0,)), ((), ())), preferred_element_type=jnp.float32)
        return acc, grad_rows

    acc, grad_blocks = lax.scan(second_pass, jnp.zeros((total, width), jnp.float32), (image_blocks, lse_blocks))
    images_f = images.astype(jnp.float32)
    texts_f = texts.astype(jnp.float32)
    matched = scale * jnp.sum(images_f * texts_f, axis=1)
    loss = (jnp.sum(lse_img) + jnp.sum(lse_txt) - 2.0 * jnp.sum(matched)) / (2.0 * total)
    grad_images = grad_blocks.reshape(total, width) - scale * texts_f
    grad_texts = acc - scale * images_f
    return loss.reshape(1), grad_images, grad_texts
```

```python
import functools
import math

import jax
import jax.numpy as jnp
from jax import lax
from jax.experimental import pallas as pl
from jax.experimental.pallas import tpu as pltpu
from jax.sharding import PartitionSpec as P

MESH = pl.DeviceIdType.MESH
F32 = jnp.float32
BF16 = jnp.bfloat16
NT = (((1,), (1,)), ((), ()))
NN = (((1,), (0,)), ((), ()))
TN = (((0,), (0,)), ((), ()))
LN2 = math.log(2.0)
NX, NY, NZ, NC = 4, 4, 8, 2
N1 = NC * NZ
N2 = NX * NY
R = 96
E = 768
M = N1 * R
N = N2 * R
LANES = 128
TILE = 4 * R


def place():
    row = lax.axis_index("row")
    col = lax.axis_index("col")
    return row // NC, lax.rem(col, NY), col // NY, lax.rem(row, NC)


def device(x, y, z, c):
    return (x * NC + c, z * NY + y)


def copy(src, dst, send, recv, to):
    return pltpu.make_async_remote_copy(
        src_ref=src, dst_ref=dst, send_sem=send, recv_sem=recv, device_id=to, device_id_type=MESH
    )


def at_rows(slot, count=R):
    return pl.ds(pl.multiple_of(slot * R, R), count)


def lse_over_first(top, total):
    high = jnp.max(top, axis=0, keepdims=True)
    return high + jnp.log2(jnp.sum(total * jnp.exp2(top - high), axis=0, keepdims=True))


def kernel(
    images, texts, scale_ref, loss_out, gi_out, gt_out,
    ibuf, tbuf, scores, weights, row_top, row_sum, col_part,
    st_i, st_t, ls_i, ls_t, p_sib, p_in, p_own, p_send, q_send, q_own, p_recv, q_recv,
    zi_s, zi_r, fi_s, fi_r, ti_s, ti_r, si_s, si_r, sj_s, sj_r, li_s, li_r, lj_s, lj_r,
    ps_s, ps_r, pz_s, pz_r, q_s, q_r,
):
    x, y, z, c = place()
    me1 = c * NZ + z
    me2 = x * NY + y
    scale = scale_ref[0]

    zs = [1, 7, 2, 6, 3, 5, 4]
    group1 = [(dz, dc) for dz in (0, 1, 7, 2, 6, 3, 5, 4) for dc in range(NC) if (dz, dc) != (0, 0)]
    group2 = [(dx, dy) for dx in (0, 1, 3, 2) for dy in (0, 1, 3, 2) if (dx, dy) != (0, 0)]

    def to1(dz, dc):
        return device(x, y, lax.rem(z + dz, NZ), lax.rem(c + dc, NC))

    def to2(dx, dy):
        return device(lax.rem(x + dx, NX), lax.rem(y + dy, NY), z, c)

    barrier = pltpu.get_barrier_semaphore()
    for d in group1:
        pl.semaphore_signal(barrier, inc=1, device_id=to1(*d), device_id_type=MESH)
    for d in group2:
        pl.semaphore_signal(barrier, inc=1, device_id=to2(*d), device_id_type=MESH)
    pl.semaphore_wait(barrier, len(group1) + len(group2))

    sib = to1(0, 1)
    z_copies = [
        copy(images, ibuf.at[at_rows(me1)], zi_s.at[k], zi_r.at[k], to1(dz, 0)) for k, dz in enumerate(zs)
    ]
    t_copies = [
        copy(texts, tbuf.at[at_rows(me2)], ti_s.at[k], ti_r.at[k], to2(*d)) for k, d in enumerate(group2)
    ]
    forwards = []
    fwd = copy(images, ibuf.at[at_rows(me1)], fi_s.at[7], fi_r.at[7], sib)
    fwd.start()
    forwards.append(fwd)
    for k in range(15):
        if k < 7:
            z_copies[k].start()
        t_copies[k].start()
    ibuf[at_rows(me1)] = images[...]
    tbuf[at_rows(me2)] = texts[...]
    matched = images[...].astype(F32) * texts[...].astype(F32)
    matched = jnp.sum(matched, axis=0, keepdims=True)
    matched = scale * functools.reduce(jnp.add, [matched[:, g * LANES:(g + 1) * LANES] for g in range(E // LANES)])
    for k, dz in enumerate(zs):
        z_copies[k].wait_recv()
        slot = c * NZ + lax.rem(z + NZ - dz, NZ)
        fwd = copy(ibuf.at[at_rows(slot)], ibuf.at[at_rows(slot)], fi_s.at[k], fi_r.at[k], sib)
        fwd.start()
        forwards.append(fwd)
    for cp in forwards:
        cp.wait_recv()
    for cp in t_copies:
        cp.wait_recv()

    scale2 = scale * (1.0 / LN2)

    @pl.loop(0, M // TILE)
    def _(t):
        i0 = pl.multiple_of(t * TILE, TILE)
        for j in range(0, N, 512):
            scores[pl.ds(i0, TILE), pl.ds(j, 512)] = scale2 * lax.dot_general(
                ibuf[pl.ds(i0, TILE), :], tbuf[pl.ds(j, 512), :], NT, preferred_element_type=F32
            )

    @pl.loop(0, M // 16)
    def _(t):
        rows = pl.ds(pl.multiple_of(t * 16, 16), 16)
        parts = [scores[rows, pl.ds(g * LANES, LANES)] for g in range(N // LANES)]
        top = functools.reduce(jnp.maximum, parts)
        row_top[rows, :] = top
        row_sum[rows, :] = functools.reduce(jnp.add, [jnp.exp2(v - top) for v in parts])

    for t in range(M // 256):
        @pl.loop(0, N // LANES)
        def _(g, t=t):
            cols = pl.ds(pl.multiple_of(g * LANES, LANES), LANES)
            parts = [scores[pl.ds(t * 256 + r * 8, 8), cols] for r in range(32)]
            top = functools.reduce(jnp.maximum, parts)
            col_part[0, pl.ds(t * 8, 8), cols] = top
            col_part[1, pl.ds(t * 8, 8), cols] = functools.reduce(jnp.add, [jnp.exp2(v - top) for v in parts])

    def fold(v):
        return jnp.concatenate([v[:, g * LANES:(g + 1) * LANES] for g in range(v.shape[1] // LANES)], axis=0)

    lse_row = lse_over_first(row_top[...].T, row_sum[...].T)
    pad = jnp.zeros((3, LANES), F32)
    st_i[me1] = jnp.concatenate([fold(lse_row), matched, pad], axis=0)
    i_copies = [
        copy(st_i.at[me1], st_i.at[me1], si_s.at[k], si_r.at[k], to1(*d)) for k, d in enumerate(group1)
    ]
    for cp in i_copies:
        cp.start()
    lse_col = lse_over_first(col_part[0], col_part[1])
    st_t[me2] = jnp.concatenate([fold(lse_col), jnp.zeros((4, LANES), F32)], axis=0)
    j_copies = [
        copy(st_t.at[me2], st_t.at[me2], sj_s.at[k], sj_r.at[k], to2(*d)) for k, d in enumerate(group2)
    ]
    for cp in j_copies:
        cp.start()

    def combine(st, groups):
        v = st[:, 0:groups, :]
        high = jnp.max(v, axis=0)
        return high + jnp.log2(jnp.sum(jnp.exp2(v - high[None]), axis=0))

    half = jnp.log2(jnp.full((1, LANES), scale * 0.5, F32))
    for cp in i_copies:
        cp.wait_recv()
    all_i = combine(st_i, M // LANES)
    all_matched = functools.reduce(jnp.add, [st_i[k, 12:13, :] for k in range(N1)])
    for g in range(M // LANES):
        row_top[pl.ds(g * LANES, LANES), :] = jnp.broadcast_to(all_i[g:g + 1] - half, (LANES, LANES)).T
    for cp in j_copies:
        cp.wait_recv()
    all_t = combine(st_t, N // LANES)
    for g in range(N // LANES):
        col_part[0, 0:1, g * LANES:(g + 1) * LANES] = all_t[g:g + 1] - half

    sum_i = LN2 * jnp.sum(all_i, axis=0, keepdims=True) - 2.0 * all_matched
    sum_t = LN2 * jnp.sum(all_t, axis=0, keepdims=True)
    ls_i[me2] = jnp.broadcast_to(sum_i, (8, LANES))
    ls_t[me1] = jnp.broadcast_to(sum_t, (8, LANES))
    loss_copies = [
        copy(ls_i.at[me2], ls_i.at[me2], li_s.at[k], li_r.at[k], to2(*d)) for k, d in enumerate(group2)
    ] + [
        copy(ls_t.at[me1], ls_t.at[me1], lj_s.at[k], lj_r.at[k], to1(*d)) for k, d in enumerate(group1)
    ]
    for cp in loss_copies:
        cp.start()

    @pl.loop(0, M // 16)
    def _(t):
        rows = pl.ds(pl.multiple_of(t * 16, 16), 16)
        shift = row_top[rows, :]
        for g in range(N // LANES):
            cols = pl.ds(g * LANES, LANES)
            v = scores[rows, cols]
            w = jnp.exp2(v - shift) + jnp.exp2(v - col_part[0, 0:1, cols])
            weights[rows, cols] = w.astype(BF16)

    def p_tile(first):
        return lax.dot_general(weights[at_rows(first, TILE), :], tbuf[...], NN, preferred_element_type=F32)

    sib_copies = []
    for h in range(2):
        p_sib[pl.ds(h * TILE, TILE)] = p_tile((1 - c) * NZ + 4 * h)
        cp = copy(
            p_sib.at[pl.ds(h * TILE, TILE)], p_in.at[pl.ds(h * TILE, TILE)], ps_s.at[h], ps_r.at[h], sib
        )
        cp.start()
        sib_copies.append(cp)

    def p_copy(slot):
        return copy(p_send.at[at_rows(slot)], p_recv.at[z], pz_s.at[slot], pz_r.at[z], device(x, y, slot, c))

    def q_copy(tx, ty):
        return copy(
            q_send.at[at_rows(tx * NY + ty)], q_recv.at[me2], q_s.at[tx * NY + ty], q_r.at[me2],
            device(tx, ty, z, c),
        )

    def do_q(dx):
        tx = lax.rem(x + dx, NX)
        cols = pl.ds(pl.multiple_of(tx * TILE, TILE), TILE)
        tile = lax.dot_general(weights[:, cols], ibuf[...], TN, preferred_element_type=F32)
        q_send[at_rows(tx * NY, TILE)] = tile.astype(BF16)
        if dx == 0:
            q_own[...] = tile
        for dy in (2, 1, 3, 0):
            if (dx, dy) != (0, 0):
                q_copy(tx, lax.rem(y + dy, NY)).start()

    def do_p(dh):
        h = lax.rem(z // 4 + dh, 2)
        rows = at_rows(4 * h, TILE)
        tile = p_tile(c * NZ + 4 * h)
        copy(p_sib.at[rows], p_in.at[rows], ps_s.at[h], ps_r.at[h], sib).wait_recv()
        tile = tile + p_in[rows]
        p_send[rows] = tile.astype(BF16)
        p_own[rows] = tile
        for q in range(4):
            slot = 4 * h + q
            if dh == 1:
                p_copy(slot).start()
            else:
                @pl.when(slot != z)
                def _(slot=slot):
                    p_copy(slot).start()

    do_q(2)
    do_p(1)
    do_q(1)
    do_p(0)
    do_q(3)
    do_q(0)

    for cp in loss_copies:
        cp.wait_recv()
    total = functools.reduce(jnp.add, [ls_i[k] for k in range(N2)]) + functools.reduce(
        jnp.add, [ls_t[k] for k in range(N1)]
    )
    loss_out[...] = total

    for d in zs:
        src = lax.rem(z + d, NZ)
        copy(p_send.at[at_rows(src)], p_recv.at[src], pz_s.at[src], pz_r.at[src], device(x, y, src, c)).wait_recv()
    for d in group2:
        src = lax.rem(x + d[0], NX) * NY + lax.rem(y + d[1], NY)
        copy(q_send.at[at_rows(src)], q_recv.at[src], q_s.at[src], q_r.at[src], to2(*d)).wait_recv()
    p_recv[z] = jnp.zeros((R, E), BF16)
    q_recv[me2] = jnp.zeros((R, E), BF16)

    @pl.loop(0, R // 16)
    def _(t):
        rows = pl.ds(pl.multiple_of(t * 16, 16), 16)
        own = pl.ds(pl.multiple_of(z * R + t * 16, 16), 16)
        gi = p_own[own] - scale * texts[rows].astype(F32)
        gi_out[rows] = functools.reduce(jnp.add, [p_recv[k, rows].astype(F32) for k in range(NZ)], gi)
        own = pl.ds(pl.multiple_of(y * R + t * 16, 16), 16)
        gt = q_own[own] - scale * images[rows].astype(F32)
        gt_out[rows] = functools.reduce(jnp.add, [q_recv[k, rows].astype(F32) for k in range(N2)], gt)

    for cp in z_copies + t_copies + forwards + i_copies + j_copies + loss_copies + sib_copies:
        cp.wait_send()
    for d in zs:
        p_copy(lax.rem(z + d, NZ)).wait_send()
    for d in group2:
        q_copy(lax.rem(x + d[0], NX), lax.rem(y + d[1], NY)).wait_send()


def local(images, texts, logit_scale):
    vmem = pl.BlockSpec(memory_space=pltpu.VMEM)
    dma = pltpu.SemaphoreType.DMA
    scratch = [
        pltpu.VMEM((M, E), BF16), pltpu.VMEM((N, E), BF16),
        pltpu.VMEM((M, N), F32), pltpu.VMEM((M, N), BF16),
        pltpu.VMEM((M, LANES), F32), pltpu.VMEM((M, LANES), F32), pltpu.VMEM((2, 48, N), F32),
        pltpu.VMEM((N1, 16, LANES), F32), pltpu.VMEM((N2, 16, LANES), F32),
        pltpu.VMEM((N2, 8, LANES), F32), pltpu.VMEM((N1, 8, LANES), F32),
        pltpu.VMEM((NZ * R, E), F32), pltpu.VMEM((NZ * R, E), F32), pltpu.VMEM((NZ * R, E), F32),
        pltpu.VMEM((NZ * R, E), BF16), pltpu.VMEM((N, E), BF16), pltpu.VMEM((TILE, E), F32),
        pltpu.VMEM((NZ, R, E), BF16), pltpu.VMEM((N2, R, E), BF16),
    ]
    sems = [7, 8, 15, 15, 15, 15, 15, 2, 8, 16]
    for n in sems:
        scratch += [dma((n,)), dma((n,))]
    sums, grad_images, grad_texts = pl.pallas_call(
        kernel,
        out_shape=(
            jax.ShapeDtypeStruct((8, LANES), F32),
            jax.ShapeDtypeStruct((R, E), F32),
            jax.ShapeDtypeStruct((R, E), F32),
        ),
        in_specs=[vmem, vmem, pl.BlockSpec(memory_space=pltpu.SMEM)],
        out_specs=(vmem, vmem, vmem),
        scratch_shapes=scratch,
        compiler_params=pltpu.CompilerParams(
            collective_id=0, has_side_effects=True, vmem_limit_bytes=56 * 2**20
        ),
    )(images, texts, logit_scale)
    pairs = R * N1 * N2
    loss = jnp.sum(sums[0:1], axis=1) / (2.0 * pairs)
    return loss, grad_images, grad_texts


def solution(mesh):
    placed = (P(("row", "col"), None), P(("row", "col"), None), P())
    return jax.shard_map(
        local,
        mesh=mesh,
        in_specs=placed,
        out_specs=(P(), P(("row", "col"), None), P(("row", "col"), None)),
        check_vma=False,
    )
```

```python
import functools
import math

import jax
import jax.numpy as jnp
from jax import lax
from jax.experimental import pallas as pl
from jax.experimental.pallas import tpu as pltpu
from jax.sharding import PartitionSpec as P

MESH = pl.DeviceIdType.MESH
F32 = jnp.float32
BF16 = jnp.bfloat16
NT = (((1,), (1,)), ((), ()))
NN = (((1,), (0,)), ((), ()))
TN = (((0,), (0,)), ((), ()))
LN2 = math.log(2.0)
NX, NY, NZ, NC = 4, 4, 8, 2
R = 96
HALF = R // 2
E = 768
SLOTS = 16
B = SLOTS * R
LANES = 128
GROUPS = B // LANES
TILE = 4 * R
CHUNK = 256

ZSTEPS = [0, 1, 7, 2, 6, 3, 5, 4]
ZPLACE = [ZSTEPS.index(d) for d in range(NZ)]
USTEPS = [0, 1, 3, 2]
UPLACE = [USTEPS.index(d) for d in range(4)]


def tree(f, parts):
    parts = list(parts)
    while len(parts) > 1:
        parts = [f(*parts[k:k + 2]) if k + 1 < len(parts) else parts[k] for k in range(0, len(parts), 2)]
    return parts[0]


def copy(src, dst, send, recv, to):
    return pltpu.make_async_remote_copy(
        src_ref=src, dst_ref=dst, send_sem=send, recv_sem=recv, device_id=to, device_id_type=MESH
    )


def rows_of(slot, count=R):
    return pl.ds(slot * R, count)


def lse_first(top, total=None):
    high = jnp.max(top, axis=0, keepdims=True)
    part = jnp.exp2(top - high)
    part = part if total is None else part * total
    return high + jnp.log2(jnp.sum(part, axis=0, keepdims=True))


def kernel(
    images, texts, scale_ref, loss_out, gi_out, gt_out,
    ibuf, tbuf, scores, weights, row_top, row_sum, col_part, col_shift,
    st_c, st_z, st_u, st_v, all_i, all_t, ls_c, ls_z, ls_x, ls_y,
    p_sib, p_in, p_own, p_send, p_recv, q_send, q_recv, q_own, r_recv,
    zi_s, zi_r, fi_s, fi_r, ti_s, ti_r, sc_s, sc_r, sz_s, sz_r, su_s, su_r, sv_s, sv_r,
    lc_s, lc_r, lz_s, lz_r, lx_s, lx_r, ly_s, ly_r, ps_s, ps_r, pz_s, pz_r, q_s, q_r, r_s, r_r,
):
    row, col = lax.axis_index("row"), lax.axis_index("col")
    x, c, z, y = row // NC, lax.rem(row, NC), col // NY, lax.rem(col, NY)
    u, v = x * (1 - c) + y * c, y * (1 - c) + x * c
    scale = scale_ref[0]

    def to(dx=0, dy=0, dz=0, dc=0):
        return (lax.rem(x + dx, NX) * NC + lax.rem(c + dc, NC), lax.rem(z + dz, NZ) * NY + lax.rem(y + dy, NY))

    def to_uv(du=0, dv=0):
        return to(dx=du * (1 - c) + dv * c, dy=dv * (1 - c) + du * c)

    sib = to(dc=1)
    started = []

    def launch(cp):
        cp.start()
        started.append(cp)
        return cp

    barrier = pltpu.get_barrier_semaphore()
    partners = [sib] + [to(dz=d) for d in ZSTEPS[1:]] + [to(dx=d) for d in USTEPS[1:]] + [to(dy=d) for d in USTEPS[1:]]
    for d in partners:
        pl.semaphore_signal(barrier, inc=1, device_id=d, device_id_type=MESH)
    pl.semaphore_wait(barrier, len(partners))

    forwards = []

    def z_copy(s, hop, h):
        k = (0 if s == 1 else 8) + (hop - 1) * 2 + h
        src = pl.ds(ZPLACE[(-s * (hop - 1)) % NZ] * R + h * HALF, HALF)
        dst = pl.ds(ZPLACE[(-s * hop) % NZ] * R + h * HALF, HALF)
        held = images.at[pl.ds(h * HALF, HALF)] if hop == 1 else ibuf.at[src]
        return copy(held, ibuf.at[dst], zi_s.at[k], zi_r.at[k], to(dz=s % NZ))

    def z_arrive(s, hop, h):
        z_copy(s, hop, h).wait_recv()
        if hop < 3 or (hop == 3 and h == (0 if s == 1 else 1)):
            launch(z_copy(s, hop + 1, h))
        k = (0 if s == 1 else 8) + (hop - 1) * 2 + h
        start = ZPLACE[(-s * hop) % NZ] * R + h * HALF
        forwards.append(launch(copy(
            ibuf.at[pl.ds(start, HALF)], ibuf.at[pl.ds(B // 2 + start, HALF)], fi_s.at[k], fi_r.at[k], sib
        )))

    def v_copy(s, hop):
        src, dst = UPLACE[(-s * (hop - 1)) % 4], UPLACE[(-s * hop) % 4]
        k = 2 if hop == 2 else (0 if s == 1 else 1)
        held = texts if hop == 1 else tbuf.at[rows_of(src)]
        return copy(held, tbuf.at[rows_of(dst)], ti_s.at[k], ti_r.at[k], to_uv(dv=s % 4))

    def u_copy(s, hop, pv):
        src, dst = 4 * UPLACE[(-s * (hop - 1)) % 4] + pv, 4 * UPLACE[(-s * hop) % 4] + pv
        k = 3 + pv * 3 + (2 if hop == 2 else (0 if s == 1 else 1))
        held = texts if hop == 1 and pv == 0 else tbuf.at[rows_of(src)]
        return copy(held, tbuf.at[rows_of(dst)], ti_s.at[k], ti_r.at[k], to_uv(du=s % 4))

    def v_arrive(s, hop):
        v_copy(s, hop).wait_recv()
        if hop == 1 and s == 1:
            launch(v_copy(1, 2))
        pv = UPLACE[(-s * hop) % 4]
        launch(u_copy(1, 1, pv))
        launch(u_copy(-1, 1, pv))

    def u_arrive(s, hop, pv):
        u_copy(s, hop, pv).wait_recv()
        if hop == 1 and s == (1 if pv % 2 == 0 else -1):
            launch(u_copy(s, 2, pv))

    for h in range(2):
        launch(z_copy(1, 1, h))
        launch(z_copy(-1, 1, h))
        if h == 0:
            launch(v_copy(1, 1))
            launch(v_copy(-1, 1))
    launch(u_copy(1, 1, 0))
    launch(u_copy(-1, 1, 0))
    forwards.append(launch(copy(images, ibuf.at[rows_of(8)], fi_s.at[16], fi_r.at[16], sib)))
    ibuf[rows_of(0)] = images[...]
    tbuf[rows_of(0)] = texts[...]
    z_events = [(s, hop, h) for hop in (1, 2, 3) for h in range(2) for s in (1, -1)] + [(1, 4, 0), (-1, 4, 1)]
    t_events = [
        (v_arrive, 1, 1), (v_arrive, -1, 1), (u_arrive, 1, 1, 0), (u_arrive, -1, 1, 0), (v_arrive, 1, 2),
        (u_arrive, 1, 1, 2), (u_arrive, -1, 1, 2), (u_arrive, 1, 1, 1), (u_arrive, -1, 1, 1), (u_arrive, 1, 2, 0),
        (u_arrive, 1, 1, 3), (u_arrive, -1, 1, 3), (u_arrive, 1, 2, 2), (u_arrive, -1, 2, 1), (u_arrive, -1, 2, 3),
    ]
    for n in range(15):
        if n < 14:
            z_arrive(*z_events[n])
        f, *what = t_events[n]
        f(*what)
    for cp in forwards:
        cp.wait_recv()

    scale2 = scale * (1.0 / LN2)

    @pl.loop(0, B // CHUNK)
    def _(t):
        r0 = pl.multiple_of(t * CHUNK, CHUNK)
        tile = scale2 * lax.dot_general(ibuf[pl.ds(r0, CHUNK), :], tbuf[...], NT, preferred_element_type=F32)
        scores[pl.ds(r0, CHUNK), :] = tile
        for r in range(0, CHUNK, 32):
            parts = [tile[r:r + 32, g * LANES:(g + 1) * LANES] for g in range(GROUPS)]
            top = tree(jnp.maximum, parts)
            row_top[pl.ds(r0 + r, 32), :] = top
            row_sum[pl.ds(r0 + r, 32), :] = tree(jnp.add, [jnp.exp2(w - top) for w in parts])
        r8 = pl.ds(pl.multiple_of(t * 8, 8), 8)
        for g in range(GROUPS):
            parts = [tile[r:r + 8, g * LANES:(g + 1) * LANES] for r in range(0, CHUNK, 8)]
            top = tree(jnp.maximum, parts)
            col_part[0, r8, g * LANES:(g + 1) * LANES] = top
            col_part[1, r8, g * LANES:(g + 1) * LANES] = tree(jnp.add, [jnp.exp2(w - top) for w in parts])

    def i_row(k):
        return lax.rem(c + k // NZ, NC) * NZ + lax.rem(z + ZSTEPS[k % NZ], NZ)

    def t_row(k):
        return lax.rem(u + USTEPS[k // 4], 4) * 4 + lax.rem(v + USTEPS[k % 4], 4)

    def spread(st, mine, steps, where, ss, rs):
        return [launch(copy(st.at[mine], st.at[mine], ss.at[k], rs.at[k], where(d))) for k, d in enumerate(steps)]

    def along_z(d):
        return to(dz=d)

    st_c[c] = jnp.zeros((SLOTS, LANES), F32)
    st_u[u] = jnp.zeros((SLOTS, LANES), F32)
    lse = lse_first(col_part[0], col_part[1])
    for k in range(SLOTS):
        st_u[u, pl.ds(t_row(k), 1), 0:R] = lse[:, k * R:(k + 1) * R]
    u_cps = spread(st_u, u, USTEPS[1:], lambda d: to_uv(du=d), su_s, su_r)
    lse = lse_first(row_top[...].T, row_sum[...].T)
    for k in range(SLOTS):
        st_c[c, pl.ds(i_row(k), 1), 0:R] = lse[:, k * R:(k + 1) * R]
    c_cp = launch(copy(st_c.at[c], st_c.at[c], sc_s.at[0], sc_r.at[0], sib))
    for cp in u_cps:
        cp.wait_recv()
    st_v[v] = lse_first(st_u[...])[0]
    v_cps = spread(st_v, v, USTEPS[1:], lambda d: to_uv(dv=d), sv_s, sv_r)
    c_cp.wait_recv()
    st_z[z] = lse_first(st_c[...])[0]
    z_cps = spread(st_z, z, ZSTEPS[1:], along_z, sz_s, sz_r)
    half = jnp.log2(jnp.full((1, LANES), scale * 0.5, F32))
    for cp in v_cps:
        cp.wait_recv()
    all_t[...] = lse_first(st_v[...])[0]
    for k in range(SLOTS):
        col_shift[0:1, k * R:(k + 1) * R] = (all_t[pl.ds(t_row(k), 1), :] - half)[:, 0:R]
    for cp in z_cps:
        cp.wait_recv()
    all_i[...] = lse_first(st_z[...])[0]
    for k in range(SLOTS):
        shift = jnp.broadcast_to(all_i[pl.ds(i_row(k), 1), :] - half, (LANES, LANES)).T
        row_top[rows_of(k), :] = shift[0:R]

    lane = lax.broadcasted_iota(jnp.int32, (1, LANES), 1)
    matched = images[...].astype(F32) * texts[...].astype(F32)
    matched = jnp.sum(matched, axis=0, keepdims=True)
    matched = tree(jnp.add, [matched[:, g * LANES:(g + 1) * LANES] for g in range(E // LANES)])
    own = all_i[pl.ds(i_row(0), 1), :] + all_t[pl.ds(t_row(0), 1), :]
    own = LN2 * jnp.where(lane < R, own, 0.0) - (2.0 * scale) * matched
    ls_c[c] = jnp.broadcast_to(own, (8, LANES))
    lc_cp = launch(copy(ls_c.at[c], ls_c.at[c], lc_s.at[0], lc_r.at[0], sib))

    def loss_z():
        lc_cp.wait_recv()
        ls_z[z] = ls_c[0] + ls_c[1]
        return spread(ls_z, z, ZSTEPS[1:], along_z, lz_s, lz_r)

    def loss_x(cps):
        for cp in cps:
            cp.wait_recv()
        ls_x[x] = functools.reduce(jnp.add, [ls_z[k] for k in range(NZ)])
        return spread(ls_x, x, USTEPS[1:], lambda d: to(dx=d), lx_s, lx_r)

    def loss_y(cps):
        for cp in cps:
            cp.wait_recv()
        ls_y[y] = functools.reduce(jnp.add, [ls_x[k] for k in range(NX)])
        return spread(ls_y, y, USTEPS[1:], lambda d: to(dy=d), ly_s, ly_r)

    def make_weights(first, count):
        @pl.loop(first // 64, (first + count) // 64)
        def _(t):
            rows = pl.ds(pl.multiple_of(t * 64, 64), 64)
            shift = row_top[rows, :]
            for g in range(GROUPS):
                cols = pl.ds(g * LANES, LANES)
                w = scores[rows, cols]
                w = jnp.exp2(w - shift) + jnp.exp2(w - col_shift[0:1, cols])
                weights[rows, cols] = w.astype(BF16)

    def p_tile(slot):
        return lax.dot_general(weights[rows_of(slot, TILE), :], tbuf[...], NN, preferred_element_type=F32)

    def sib_copy(h):
        rows = pl.ds(h * TILE, TILE)
        return copy(p_sib.at[rows], p_in.at[rows], ps_s.at[h], ps_r.at[h], sib)

    def do_sib(h):
        p_sib[pl.ds(h * TILE, TILE)] = p_tile(8 + 4 * h)
        launch(sib_copy(h))

    def p_copy(p):
        back = ZPLACE[-ZSTEPS[p] % NZ]
        return copy(p_send.at[rows_of(p)], p_recv.at[back], pz_s.at[p], pz_r.at[p], to(dz=ZSTEPS[p]))

    def do_own(h):
        rows = pl.ds(h * TILE, TILE)
        tile = p_tile(4 * h)
        sib_copy(h).wait_recv()
        tile = tile + p_in[rows]
        p_send[rows] = tile.astype(BF16)
        if h == 0:
            p_own[...] = tile[0:R]
        for p in range(4 * h + 3, 4 * h - 1, -1):
            if p:
                launch(p_copy(p))

    def q_copy(p):
        back = UPLACE[-USTEPS[p] % 4] - 1
        return copy(q_send.at[p - 1], q_recv.at[back], q_s.at[p - 1], q_r.at[p - 1], to_uv(du=USTEPS[p]))

    def do_q(p):
        tile = lax.dot_general(weights[:, rows_of(4 * p, TILE)], ibuf[...], TN, preferred_element_type=F32)
        if p:
            q_send[p - 1] = tile.astype(BF16)
            launch(q_copy(p))
        else:
            q_own[...] = tile

    def r_copy(p):
        back = UPLACE[-USTEPS[p] % 4] - 1
        return copy(q_own.at[rows_of(p)], r_recv.at[back], r_s.at[p - 1], r_r.at[p - 1], to_uv(dv=USTEPS[p]))

    make_weights(8 * R + TILE, TILE)
    loss_cps = loss_z()
    do_sib(1)
    make_weights(TILE, TILE)
    loss_cps = loss_x(loss_cps)
    do_own(1)
    make_weights(0, TILE)
    make_weights(8 * R, TILE)
    loss_cps = loss_y(loss_cps)
    do_q(3)
    do_q(1)
    do_q(2)
    do_sib(0)
    do_own(0)
    do_q(0)
    for cp in loss_cps:
        cp.wait_recv()
    total = functools.reduce(jnp.add, [ls_y[k] for k in range(NY)])
    loss_out[0] = jnp.sum(total[0:1]) * (1.0 / (2.0 * R * NX * NY * NZ * NC))

    for p in range(1, 4):
        q_copy(p).wait_recv()
    for p in (3, 1, 2, 0):
        @pl.loop(0, R // 32)
        def _(t, p=p):
            rows = pl.ds(pl.multiple_of(p * R + t * 32, 32), 32)
            q_own[rows] = functools.reduce(jnp.add, [q_recv[k, rows].astype(F32) for k in range(3)], q_own[rows])
        if p:
            launch(r_copy(p))
    for p in range(1, 8):
        p_copy(p).wait_recv()

    @pl.loop(0, R // 16)
    def _(t):
        rows = pl.ds(pl.multiple_of(t * 16, 16), 16)
        gi = p_own[rows] - scale * texts[rows].astype(F32)
        gi_out[rows] = functools.reduce(jnp.add, [p_recv[k, rows].astype(F32) for k in range(1, NZ)], gi)

    for p in range(1, 4):
        r_copy(p).wait_recv()

    @pl.loop(0, R // 16)
    def _(t):
        rows = pl.ds(pl.multiple_of(t * 16, 16), 16)
        gt = q_own[rows] - scale * images[rows].astype(F32)
        gt_out[rows] = functools.reduce(jnp.add, [r_recv[k, rows] for k in range(3)], gt)

    for cp in started:
        cp.wait_send()


def local(images, texts, logit_scale):
    vmem = pl.BlockSpec(memory_space=pltpu.VMEM)
    smem = pl.BlockSpec(memory_space=pltpu.SMEM)
    dma = pltpu.SemaphoreType.DMA
    scratch = [
        pltpu.VMEM((B, E), BF16), pltpu.VMEM((B, E), BF16), pltpu.VMEM((B, B), F32), pltpu.VMEM((B, B), BF16),
        pltpu.VMEM((B, LANES), F32), pltpu.VMEM((B, LANES), F32),
        pltpu.VMEM((2, 8 * (B // CHUNK), B), F32), pltpu.VMEM((8, B), F32),
    ]
    scratch += [pltpu.VMEM((n, SLOTS, LANES), F32) for n in (NC, NZ, 4, 4)]
    scratch += [pltpu.VMEM((SLOTS, LANES), F32)] * 2
    scratch += [pltpu.VMEM((n, 8, LANES), F32) for n in (NC, NZ, NX, NY)]
    scratch += [
        pltpu.VMEM((NZ * R, E), F32), pltpu.VMEM((NZ * R, E), F32), pltpu.VMEM((R, E), F32),
        pltpu.VMEM((NZ * R, E), BF16), pltpu.VMEM((NZ, R, E), BF16),
        pltpu.VMEM((3, TILE, E), BF16), pltpu.VMEM((3, TILE, E), BF16), pltpu.VMEM((TILE, E), F32),
        pltpu.VMEM((3, R, E), F32),
    ]
    for n in (16, 17, 15, 1, 7, 3, 3, 1, 7, 3, 3, 2, 8, 3, 3):
        scratch += [dma((n,)), dma((n,))]
    return pl.pallas_call(
        kernel,
        out_shape=(
            jax.ShapeDtypeStruct((1,), F32),
            jax.ShapeDtypeStruct((R, E), F32),
            jax.ShapeDtypeStruct((R, E), F32),
        ),
        in_specs=[vmem, vmem, smem],
        out_specs=(smem, vmem, vmem),
        scratch_shapes=scratch,
        compiler_params=pltpu.CompilerParams(
            collective_id=0, has_side_effects=True, vmem_limit_bytes=56 * 2**20
        ),
    )(images, texts, logit_scale)


def solution(mesh):
    placed = (P(("row", "col"), None), P(("row", "col"), None), P())
    return jax.shard_map(
        local,
        mesh=mesh,
        in_specs=placed,
        out_specs=(P(), P(("row", "col"), None), P(("row", "col"), None)),
        check_vma=False,
    )
```

```python
import functools
import math

import jax
import jax.numpy as jnp
from jax import lax
from jax.experimental import pallas as pl
from jax.experimental.pallas import tpu as pltpu
from jax.sharding import PartitionSpec as P

MESH = pl.DeviceIdType.MESH
F32 = jnp.float32
BF16 = jnp.bfloat16
NT = (((1,), (1,)), ((), ()))
NN = (((1,), (0,)), ((), ()))
TN = (((0,), (0,)), ((), ()))
LN2 = math.log(2.0)
NX, NY, NZ, NC = 4, 4, 8, 2
R = 96
HALF = R // 2
PIECES = 3
PIECE = R // PIECES
E = 768
SLOTS = 16
B = SLOTS * R
LANES = 128
GROUPS = B // LANES
TILE = 4 * R
CHUNK = 256

ZSTEPS = [0, 7, 2, 6, 1, 3, 5, 4]
ZPLACE = [ZSTEPS.index(d) for d in range(NZ)]
USTEPS = [0, 1, 3, 2]
UPLACE = [USTEPS.index(d) for d in range(4)]


def tree(f, parts):
    parts = list(parts)
    while len(parts) > 1:
        parts = [f(*parts[k:k + 2]) if k + 1 < len(parts) else parts[k] for k in range(0, len(parts), 2)]
    return parts[0]


def copy(src, dst, send, recv, to):
    return pltpu.make_async_remote_copy(
        src_ref=src, dst_ref=dst, send_sem=send, recv_sem=recv, device_id=to, device_id_type=MESH
    )


def rows_of(slot, count=R):
    return pl.ds(slot * R, count)


def lse_first(top, total=None):
    high = jnp.max(top, axis=0, keepdims=True)
    part = jnp.exp2(top - high)
    part = part if total is None else part * total
    return high + jnp.log2(jnp.sum(part, axis=0, keepdims=True))


def kernel(
    images, texts, scale_ref, loss_out, gi_out, gt_out,
    ibuf, tbuf, scores, weights, row_top, row_sum, col_part, col_shift,
    st_c, st_z, st_u, st_v, all_i, all_t, ls_c, ls_z, ls_x, ls_y,
    p_sib, p_in, p_own, p_send, p_recv, f_recv, h_recv, q_send, q_recv, q_own, r_recv,
    zi_s, zi_r, fi_s, fi_r, ti_s, ti_r, sc_s, sc_r, sz_s, sz_r, su_s, su_r, sv_s, sv_r,
    lc_s, lc_r, lz_s, lz_r, lx_s, lx_r, ly_s, ly_r, ps_s, ps_r, pz_s, pz_r, q_s, q_r, r_s, r_r,
):
    row, col = lax.axis_index("row"), lax.axis_index("col")
    x, c, z, y = row // NC, lax.rem(row, NC), col // NY, lax.rem(col, NY)
    u, v = x * (1 - c) + y * c, y * (1 - c) + x * c
    scale = scale_ref[0]

    def to(dx=0, dy=0, dz=0, dc=0):
        return (lax.rem(x + dx, NX) * NC + lax.rem(c + dc, NC), lax.rem(z + dz, NZ) * NY + lax.rem(y + dy, NY))

    def to_uv(du=0, dv=0):
        return to(dx=du * (1 - c) + dv * c, dy=dv * (1 - c) + du * c)

    sib = to(dc=1)
    started = []

    def launch(cp):
        cp.start()
        started.append(cp)
        return cp

    barrier = pltpu.get_barrier_semaphore()
    partners = [sib] + [to(dz=d) for d in ZSTEPS[1:]] + [to(dx=d) for d in USTEPS[1:]] + [to(dy=d) for d in USTEPS[1:]]
    for d in partners:
        pl.semaphore_signal(barrier, inc=1, device_id=d, device_id_type=MESH)
    pl.semaphore_wait(barrier, len(partners))

    def z_copy(s, hop, i):
        k = (0 if s == 1 else 12) + (hop - 1) * PIECES + i
        src = pl.ds(ZPLACE[(-s * (hop - 1)) % NZ] * R + i * PIECE, PIECE)
        dst = pl.ds(ZPLACE[(-s * hop) % NZ] * R + i * PIECE, PIECE)
        held = images.at[pl.ds(i * PIECE, PIECE)] if hop == 1 else ibuf.at[src]
        return copy(held, ibuf.at[dst], zi_s.at[k], zi_r.at[k], to(dz=s % NZ))

    def last_hop(s):
        return (0, 1) if s == 1 else (2,)

    def z_arrive(s, hop):
        for i in last_hop(s) if hop == 4 else range(PIECES):
            z_copy(s, hop, i).wait_recv()
            if hop < 3 or (hop == 3 and i in last_hop(s)):
                launch(z_copy(s, hop + 1, i))
        if hop < 4:
            forward(ZPLACE[(-s * hop) % NZ] * R, R)
        else:
            forward(ZPLACE[4] * R + last_hop(s)[0] * PIECE, PIECE * len(last_hop(s)))

    forwards = []

    def forward(start, count):
        k = len(forwards)
        src = images if start == 0 else ibuf.at[pl.ds(start, count)]
        forwards.append(launch(copy(src, ibuf.at[pl.ds(B // 2 + start, count)], fi_s.at[k], fi_r.at[k], sib)))

    def v_copy(s, hop):
        src, dst = UPLACE[(-s * (hop - 1)) % 4], UPLACE[(-s * hop) % 4]
        k = 2 if hop == 2 else (0 if s == 1 else 1)
        held = texts if hop == 1 else tbuf.at[rows_of(src)]
        return copy(held, tbuf.at[rows_of(dst)], ti_s.at[k], ti_r.at[k], to_uv(dv=s % 4))

    def u_copy(s, hop, pv):
        src, dst = 4 * UPLACE[(-s * (hop - 1)) % 4] + pv, 4 * UPLACE[(-s * hop) % 4] + pv
        k = 3 + pv * 3 + (2 if hop == 2 else (0 if s == 1 else 1))
        held = texts if hop == 1 and pv == 0 else tbuf.at[rows_of(src)]
        return copy(held, tbuf.at[rows_of(dst)], ti_s.at[k], ti_r.at[k], to_uv(du=s % 4))

    def v_arrive(s, hop):
        v_copy(s, hop).wait_recv()
        if hop == 1 and s == 1:
            launch(v_copy(1, 2))
        pv = UPLACE[(-s * hop) % 4]
        launch(u_copy(1, 1, pv))
        launch(u_copy(-1, 1, pv))

    def u_arrive(s, hop, pv):
        u_copy(s, hop, pv).wait_recv()
        if hop == 1 and s == (1 if pv % 2 == 0 else -1):
            launch(u_copy(s, 2, pv))

    for i in range(PIECES):
        launch(z_copy(1, 1, i))
        launch(z_copy(-1, 1, i))
        if i == 0:
            launch(v_copy(1, 1))
            launch(v_copy(-1, 1))
    launch(u_copy(1, 1, 0))
    launch(u_copy(-1, 1, 0))
    forward(0, R)
    ibuf[rows_of(0)] = images[...]
    tbuf[rows_of(0)] = texts[...]
    z_arrive(1, 1)
    z_arrive(-1, 1)
    v_arrive(1, 1)
    v_arrive(-1, 1)
    u_arrive(1, 1, 0)
    u_arrive(-1, 1, 0)
    z_arrive(1, 2)
    z_arrive(-1, 2)
    v_arrive(1, 2)
    for pv in (2, 1):
        u_arrive(1, 1, pv)
        u_arrive(-1, 1, pv)
    z_arrive(1, 3)
    z_arrive(-1, 3)
    u_arrive(1, 1, 3)
    u_arrive(-1, 1, 3)
    for cp in forwards:
        cp.wait_recv()

    scale2 = scale * (1.0 / LN2)
    late = 7 * R
    early_n = 12 * R

    def score_block(r0, part, count, c0, width, merge):
        rows = pl.ds(r0, count)
        tile = scale2 * lax.dot_general(ibuf[rows, :], tbuf[pl.ds(c0, width), :], NT, preferred_element_type=F32)
        scores[rows, pl.ds(c0, width)] = tile
        for r in range(0, count, 32):
            sub = pl.ds(r0 + r, 32)
            parts = [tile[r:r + 32, g:g + LANES] for g in range(0, width, LANES)]
            top = tree(jnp.maximum, parts)
            if merge:
                old = row_top[sub, :]
                top = jnp.maximum(top, old)
            total = tree(jnp.add, [jnp.exp2(w - top) for w in parts])
            if merge:
                total = total + row_sum[sub, :] * jnp.exp2(old - top)
            row_top[sub, :] = top
            row_sum[sub, :] = total
        for g in range(0, width, LANES):
            parts = [tile[r:r + 8, g:g + LANES] for r in range(0, count, 8)]
            top = tree(jnp.maximum, parts)
            col_part[0, part, c0 + g:c0 + g + LANES] = top
            col_part[1, part, c0 + g:c0 + g + LANES] = tree(jnp.add, [jnp.exp2(w - top) for w in parts])

    def eight(t):
        return pl.ds(pl.multiple_of(t * 8, 8), 8)

    @pl.loop(0, 6)
    def _(t):
        r0 = pl.multiple_of((t // 3) * (B // 2) + lax.rem(t, 3) * (late // 3), 32)
        score_block(r0, eight(t), late // 3, 0, early_n, False)

    waiting = len(forwards)
    z_arrive(1, 4)
    z_arrive(-1, 4)
    for pv in range(4):
        u_arrive(1 if pv % 2 == 0 else -1, 2, pv)

    for cp in forwards[waiting:]:
        cp.wait_recv()

    @pl.loop(0, 2)
    def _(t):
        score_block(pl.multiple_of(t * (B // 2) + late, 32), eight(6 + t), R, 0, early_n, False)

    @pl.loop(0, B // CHUNK)
    def _(t):
        score_block(pl.multiple_of(t * CHUNK, CHUNK), eight(t), CHUNK, early_n, B - early_n, True)

    def i_row(k):
        return lax.rem(c + k // NZ, NC) * NZ + lax.rem(z + ZSTEPS[k % NZ], NZ)

    def t_row(k):
        return lax.rem(u + USTEPS[k // 4], 4) * 4 + lax.rem(v + USTEPS[k % 4], 4)

    def spread(st, mine, steps, where, ss, rs):
        return [launch(copy(st.at[mine], st.at[mine], ss.at[k], rs.at[k], where(d))) for k, d in enumerate(steps)]

    def along_z(d):
        return to(dz=d)

    matched = images[...].astype(F32) * texts[...].astype(F32)
    matched = jnp.sum(matched, axis=0, keepdims=True)
    matched = tree(jnp.add, [matched[:, g * LANES:(g + 1) * LANES] for g in range(E // LANES)])
    st_c[c] = jnp.zeros((SLOTS + 8, LANES), F32)
    st_c[c, SLOTS:SLOTS + 1, :] = matched
    st_u[u] = jnp.zeros((SLOTS, LANES), F32)
    lse = jnp.concatenate([
        lse_first(col_part[0, :, 0:early_n], col_part[1, :, 0:early_n]),
        lse_first(col_part[0, 0:48, early_n:B], col_part[1, 0:48, early_n:B]),
    ], axis=1)
    for k in range(SLOTS):
        st_u[u, pl.ds(t_row(k), 1), 0:R] = lse[:, k * R:(k + 1) * R]
    u_cps = spread(st_u, u, USTEPS[1:], lambda d: to_uv(du=d), su_s, su_r)
    lse = lse_first(row_top[...].T, row_sum[...].T)
    for k in range(SLOTS):
        st_c[c, pl.ds(i_row(k), 1), 0:R] = lse[:, k * R:(k + 1) * R]
    c_cp = launch(copy(st_c.at[c], st_c.at[c], sc_s.at[0], sc_r.at[0], sib))
    for cp in u_cps:
        cp.wait_recv()
    st_v[v] = lse_first(st_u[...])[0]
    v_cps = spread(st_v, v, USTEPS[1:], lambda d: to_uv(dv=d), sv_s, sv_r)
    c_cp.wait_recv()
    st_z[z, 0:SLOTS] = lse_first(st_c[:, 0:SLOTS])[0]
    st_z[z, SLOTS:] = st_c[0, SLOTS:] + st_c[1, SLOTS:]
    z_cps = spread(st_z, z, ZSTEPS[1:], along_z, sz_s, sz_r)
    half = jnp.log2(jnp.full((1, LANES), scale * 0.5, F32))
    for cp in v_cps:
        cp.wait_recv()
    all_t[...] = lse_first(st_v[...])[0]
    for k in range(SLOTS):
        col_shift[0:1, k * R:(k + 1) * R] = (all_t[pl.ds(t_row(k), 1), :] - half)[:, 0:R]
    for cp in z_cps:
        cp.wait_recv()
    all_i[...] = lse_first(st_z[:, 0:SLOTS])[0]
    for k in range(SLOTS):
        shift = jnp.broadcast_to(all_i[pl.ds(i_row(k), 1), :] - half, (LANES, LANES)).T
        row_top[rows_of(k), :] = shift[0:R]

    def own_sum(v):
        lane = lax.broadcasted_iota(jnp.int32, (1, LANES), 1)
        return jnp.where(lane < R, LN2 * jnp.sum(v, axis=0, keepdims=True), 0.0)

    def total_of(st, n):
        return functools.reduce(jnp.add, [st[k] for k in range(n)])

    all_matched = functools.reduce(jnp.add, [st_z[k, SLOTS:SLOTS + 1, :] for k in range(NZ)])
    ls_x[x] = jnp.broadcast_to(own_sum(all_i[...]) - (2.0 * scale) * all_matched, (8, LANES))
    ls_c[c] = jnp.broadcast_to(own_sum(all_t[...]), (8, LANES))
    lx_cps = spread(ls_x, x, USTEPS[1:], lambda d: to(dx=d), lx_s, lx_r)
    lc_cps = [launch(copy(ls_c.at[c], ls_c.at[c], lc_s.at[0], lc_r.at[0], sib))]

    def make_weights(first, count):
        @pl.loop(first // 64, (first + count) // 64)
        def _(t):
            rows = pl.ds(pl.multiple_of(t * 64, 64), 64)
            shift = row_top[rows, :]
            for g in range(GROUPS):
                cols = pl.ds(g * LANES, LANES)
                w = scores[rows, cols]
                w = jnp.exp2(w - shift) + jnp.exp2(w - col_shift[0:1, cols])
                weights[rows, cols] = w.astype(BF16)

    def p_tile(slot):
        return lax.dot_general(weights[rows_of(slot, TILE), :], tbuf[...], NN, preferred_element_type=F32)

    def sib_copy(h):
        rows = pl.ds(h * TILE, TILE)
        return copy(p_sib.at[rows], p_in.at[rows], ps_s.at[h], ps_r.at[h], sib)

    def do_sib(h):
        p_sib[pl.ds(h * TILE, TILE)] = p_tile(8 + 4 * h)
        launch(sib_copy(h))

    def p_copy(k):
        if k == 0 or k == 7:
            dz, rows = (2, 0) if k == 0 else (6, HALF)
            src = p_send.at[pl.ds(7 * R + rows, HALF)]
            return copy(src, h_recv.at[rows // HALF], pz_s.at[k], pz_r.at[k], to(dz=dz))
        src = p_send.at[rows_of(k)]
        if k in (5, 6):
            return copy(src, f_recv.at[k - 5], pz_s.at[k], pz_r.at[k], to(dz=1 if k == 5 else 7))
        return copy(src, p_recv.at[k - 1], pz_s.at[k], pz_r.at[k], to(dz=ZSTEPS[k]))

    def own_tile(h):
        tile = p_tile(4 * h)
        sib_copy(h).wait_recv()
        return tile + p_in[pl.ds(h * TILE, TILE)]

    def do_far():
        p_send[pl.ds(TILE, TILE)] = own_tile(1).astype(BF16)
        for k in (5, 6, 0, 7, 4):
            launch(p_copy(k))

    def do_near():
        tile = own_tile(0)
        p_own[...] = tile
        p_send[rows_of(1)] = tile[R:2 * R].astype(BF16)
        launch(p_copy(1))

    def do_merge():
        for k in (5, 0, 6, 7):
            p_copy(k).wait_recv()
        for i in range(2):
            @pl.loop(0, HALF // 16)
            def _(t, i=i):
                near = pl.multiple_of(t * 16, 16)
                for base, with_half in ((i * HALF, True), (HALF - i * HALF, False)):
                    rows = pl.ds(base + near, 16)
                    out = pl.ds((2 + i) * R + base + near, 16)
                    w = p_own[out] + f_recv[i, rows].astype(F32)
                    if with_half:
                        w = w + h_recv[i, pl.ds(near, 16)].astype(F32)
                    p_send[out] = w.astype(BF16)
            launch(p_copy(2 + i))

    def q_copy(p, pv):
        k = (p - 1) * 4 + pv
        return copy(q_send.at[p - 1, rows_of(pv)], q_recv.at[p - 1, rows_of(pv)], q_s.at[k], q_r.at[k], to_uv(du=USTEPS[p]))

    def do_q(p):
        tile = lax.dot_general(weights[:, rows_of(4 * p, TILE)], ibuf[...], TN, preferred_element_type=F32)
        if p:
            q_send[p - 1] = tile.astype(BF16)
            for pv in (3, 1, 2, 0):
                launch(q_copy(p, pv))
        else:
            q_own[...] = tile

    def r_copy(p):
        return copy(q_own.at[rows_of(p)], r_recv.at[p - 1], r_s.at[p - 1], r_r.at[p - 1], to_uv(dv=USTEPS[p]))

    make_weights(0, B)
    for cp in lx_cps + lc_cps:
        cp.wait_recv()
    ls_y[y] = total_of(ls_x, NX)
    ls_z[z] = total_of(ls_c, NC)
    ly_cps = spread(ls_y, y, USTEPS[1:], lambda d: to(dy=d), ly_s, ly_r)
    lz_cps = spread(ls_z, z, ZSTEPS[1:], along_z, lz_s, lz_r)
    do_q(3)
    do_sib(1)
    do_q(1)
    do_far()
    do_q(2)
    do_sib(0)
    do_q(0)
    do_near()
    do_merge()
    for cp in ly_cps + lz_cps:
        cp.wait_recv()
    total = total_of(ls_y, NY) + total_of(ls_z, NZ)
    loss_out[0] = jnp.sum(total[0:1]) * (1.0 / (2.0 * R * NX * NY * NZ * NC))

    for pv in (3, 1, 2, 0):
        for p in range(1, 4):
            q_copy(p, pv).wait_recv()

        @pl.loop(0, R // 32)
        def _(t, pv=pv):
            rows = pl.ds(pl.multiple_of(pv * R + t * 32, 32), 32)
            q_own[rows] = functools.reduce(jnp.add, [q_recv[k, rows].astype(F32) for k in range(3)], q_own[rows])
        if pv:
            launch(r_copy(pv))
    for k in range(1, 5):
        p_copy(k).wait_recv()

    @pl.loop(0, R // 16)
    def _(t):
        rows = pl.ds(pl.multiple_of(t * 16, 16), 16)
        gi = p_own[rows] - scale * texts[rows].astype(F32)
        gi_out[rows] = functools.reduce(jnp.add, [p_recv[k, rows].astype(F32) for k in range(4)], gi)

    for p in range(1, 4):
        r_copy(p).wait_recv()

    @pl.loop(0, R // 16)
    def _(t):
        rows = pl.ds(pl.multiple_of(t * 16, 16), 16)
        gt = q_own[rows] - scale * images[rows].astype(F32)
        gt_out[rows] = functools.reduce(jnp.add, [r_recv[k, rows] for k in range(3)], gt)

    for cp in started:
        cp.wait_send()


def local(images, texts, logit_scale):
    vmem = pl.BlockSpec(memory_space=pltpu.VMEM)
    smem = pl.BlockSpec(memory_space=pltpu.SMEM)
    dma = pltpu.SemaphoreType.DMA
    scratch = [
        pltpu.VMEM((B, E), BF16), pltpu.VMEM((B, E), BF16), pltpu.VMEM((B, B), F32), pltpu.VMEM((B, B), BF16),
        pltpu.VMEM((B, LANES), F32), pltpu.VMEM((B, LANES), F32),
        pltpu.VMEM((2, 64, B), F32), pltpu.VMEM((8, B), F32),
    ]
    scratch += [pltpu.VMEM((n, SLOTS + 8, LANES), F32) for n in (NC, NZ)]
    scratch += [pltpu.VMEM((n, SLOTS, LANES), F32) for n in (4, 4)]
    scratch += [pltpu.VMEM((SLOTS, LANES), F32)] * 2
    scratch += [pltpu.VMEM((n, 8, LANES), F32) for n in (NC, NZ, NX, NY)]
    scratch += [
        pltpu.VMEM((NZ * R, E), F32), pltpu.VMEM((NZ * R, E), F32), pltpu.VMEM((TILE, E), F32),
        pltpu.VMEM((NZ * R, E), BF16), pltpu.VMEM((4, R, E), BF16),
        pltpu.VMEM((2, R, E), BF16), pltpu.VMEM((2, HALF, E), BF16),
        pltpu.VMEM((3, TILE, E), BF16), pltpu.VMEM((3, TILE, E), BF16), pltpu.VMEM((TILE, E), F32),
        pltpu.VMEM((3, R, E), F32),
    ]
    for n in (24, 9, 15, 1, 7, 3, 3, 1, 7, 3, 3, 2, 8, 12, 3):
        scratch += [dma((n,)), dma((n,))]
    return pl.pallas_call(
        kernel,
        out_shape=(
            jax.ShapeDtypeStruct((1,), F32),
            jax.ShapeDtypeStruct((R, E), F32),
            jax.ShapeDtypeStruct((R, E), F32),
        ),
        in_specs=[vmem, vmem, smem],
        out_specs=(smem, vmem, vmem),
        scratch_shapes=scratch,
        compiler_params=pltpu.CompilerParams(
            collective_id=0, has_side_effects=True, vmem_limit_bytes=56 * 2**20
        ),
    )(images, texts, logit_scale)


def solution(mesh):
    placed = (P(("row", "col"), None), P(("row", "col"), None), P())
    return jax.shard_map(
        local,
        mesh=mesh,
        in_specs=placed,
        out_specs=(P(), P(("row", "col"), None), P(("row", "col"), None)),
        check_vma=False,
    )
```

```python
import functools
import math

import jax
import jax.numpy as jnp
from jax import lax
from jax.experimental import pallas as pl
from jax.experimental.pallas import tpu as pltpu
from jax.sharding import PartitionSpec as P

MESH = pl.DeviceIdType.MESH
F32 = jnp.float32
BF16 = jnp.bfloat16
NT = (((1,), (1,)), ((), ()))
NN = (((1,), (0,)), ((), ()))
TN = (((0,), (0,)), ((), ()))
LN2 = math.log(2.0)
NX, NY, NZ, NC = 4, 4, 8, 2
R = 96
HALF = R // 2
PIECES = 3
PIECE = R // PIECES
E = 768
SLOTS = 16
B = SLOTS * R
LANES = 128
GROUPS = B // LANES
TILE = 4 * R
CHUNK = 256

ZSTEPS = [0, 7, 2, 6, 1, 3, 5, 4]
ZPLACE = [ZSTEPS.index(d) for d in range(NZ)]
USTEPS = [0, 1, 3, 2]
UPLACE = [USTEPS.index(d) for d in range(4)]


def tree(f, parts):
    parts = list(parts)
    while len(parts) > 1:
        parts = [f(*parts[k:k + 2]) if k + 1 < len(parts) else parts[k] for k in range(0, len(parts), 2)]
    return parts[0]


def copy(src, dst, send, recv, to):
    return pltpu.make_async_remote_copy(
        src_ref=src, dst_ref=dst, send_sem=send, recv_sem=recv, device_id=to, device_id_type=MESH
    )


def rows_of(slot, count=R):
    return pl.ds(slot * R, count)


def lse_first(top, total=None):
    high = jnp.max(top, axis=0, keepdims=True)
    part = jnp.exp2(top - high)
    part = part if total is None else part * total
    return high + jnp.log2(jnp.sum(part, axis=0, keepdims=True))


def kernel(
    images, texts, scale_ref, loss_out, gi_out, gt_out,
    ibuf, tbuf, scores, weights, row_top, row_sum, col_part, col_shift,
    row_lse, row_shift, st_c, st_z, st_t, all_i, all_t, ls_c, ls_z, ls_x, ls_y,
    p_sib, p_in, p_own, p_send, p_recv, f_recv, h_recv, q_send, q_recv, q_own, r_recv,
    zi_s, zi_r, fi_s, fi_r, ti_s, ti_r, sc_s, sc_r, sz_s, sz_r, st_s, st_r,
    lc_s, lc_r, lz_s, lz_r, lx_s, lx_r, ly_s, ly_r, ps_s, ps_r, pz_s, pz_r, q_s, q_r, r_s, r_r,
):
    row, col = lax.axis_index("row"), lax.axis_index("col")
    x, c, z, y = row // NC, lax.rem(row, NC), col // NY, lax.rem(col, NY)
    u, v = x * (1 - c) + y * c, y * (1 - c) + x * c
    scale = scale_ref[0]

    def to(dx=0, dy=0, dz=0, dc=0):
        return (lax.rem(x + dx, NX) * NC + lax.rem(c + dc, NC), lax.rem(z + dz, NZ) * NY + lax.rem(y + dy, NY))

    def to_uv(du=0, dv=0):
        return to(dx=du * (1 - c) + dv * c, dy=dv * (1 - c) + du * c)

    sib = to(dc=1)
    started = []

    def launch(cp):
        cp.start()
        started.append(cp)
        return cp

    barrier = pltpu.get_barrier_semaphore()
    uv_steps = [(du, dv) for du in USTEPS for dv in USTEPS if (du, dv) != (0, 0)]
    partners = [sib] + [to(dz=d) for d in ZSTEPS[1:]] + [to(dx=du, dy=dv) for du, dv in uv_steps]
    for d in partners:
        pl.semaphore_signal(barrier, inc=1, device_id=d, device_id_type=MESH)
    pl.semaphore_wait(barrier, len(partners))

    def z_copy(s, hop, i):
        k = (0 if s == 1 else 12) + (hop - 1) * PIECES + i
        src = pl.ds(ZPLACE[(-s * (hop - 1)) % NZ] * R + i * PIECE, PIECE)
        dst = pl.ds(ZPLACE[(-s * hop) % NZ] * R + i * PIECE, PIECE)
        held = images.at[pl.ds(i * PIECE, PIECE)] if hop == 1 else ibuf.at[src]
        return copy(held, ibuf.at[dst], zi_s.at[k], zi_r.at[k], to(dz=s % NZ))

    def last_hop(s):
        return (0, 1) if s == 1 else (2,)

    def z_arrive(s, hop):
        for i in last_hop(s) if hop == 4 else range(PIECES):
            z_copy(s, hop, i).wait_recv()
            if hop < 3 or (hop == 3 and i in last_hop(s)):
                launch(z_copy(s, hop + 1, i))
        if hop < 4:
            forward(ZPLACE[(-s * hop) % NZ] * R, R)
        else:
            forward(ZPLACE[4] * R + last_hop(s)[0] * PIECE, PIECE * len(last_hop(s)))

    forwards = []

    def forward(start, count):
        k = len(forwards)
        src = images if start == 0 else ibuf.at[pl.ds(start, count)]
        forwards.append(launch(copy(src, ibuf.at[pl.ds(B // 2 + start, count)], fi_s.at[k], fi_r.at[k], sib)))

    def v_copy(s, hop):
        k = 2 if hop == 2 else (0 if s == 1 else 1)
        dst = rows_of(UPLACE[(-s * hop) % 4])
        return copy(texts, tbuf.at[dst], ti_s.at[k], ti_r.at[k], to_uv(dv=s * hop % 4))

    def u_copy(s, hop, pv):
        src, dst = 4 * UPLACE[(-s * (hop - 1)) % 4] + pv, 4 * UPLACE[(-s * hop) % 4] + pv
        k = 3 + pv * 3 + (2 if hop == 2 else (0 if s == 1 else 1))
        held = texts if hop == 1 and pv == 0 else tbuf.at[rows_of(src)]
        return copy(held, tbuf.at[rows_of(dst)], ti_s.at[k], ti_r.at[k], to_uv(du=s % 4))

    def v_arrive(s, hop):
        v_copy(s, hop).wait_recv()
        pv = UPLACE[(-s * hop) % 4]
        launch(u_copy(1, 1, pv))
        launch(u_copy(-1, 1, pv))

    def u_arrive(s, hop, pv):
        u_copy(s, hop, pv).wait_recv()
        if hop == 1 and s == (1 if pv % 2 == 0 else -1):
            launch(u_copy(s, 2, pv))

    for i in range(PIECES):
        launch(z_copy(1, 1, i))
        launch(z_copy(-1, 1, i))
        if i == 0:
            launch(v_copy(1, 1))
            launch(v_copy(-1, 1))
    launch(v_copy(1, 2))
    launch(u_copy(1, 1, 0))
    launch(u_copy(-1, 1, 0))
    forward(0, R)
    ibuf[rows_of(0)] = images[...]
    tbuf[rows_of(0)] = texts[...]
    matched = images[...].astype(F32) * texts[...].astype(F32)
    matched = jnp.sum(matched, axis=0, keepdims=True)
    matched = tree(jnp.add, [matched[:, g:g + LANES - R] for g in range(0, E, LANES - R)])
    z_arrive(1, 1)
    z_arrive(-1, 1)
    v_arrive(1, 1)
    v_arrive(-1, 1)
    u_arrive(1, 1, 0)
    u_arrive(-1, 1, 0)
    z_arrive(1, 2)
    z_arrive(-1, 2)
    v_arrive(1, 2)
    for pv in (2, 1):
        u_arrive(1, 1, pv)
        u_arrive(-1, 1, pv)
    z_arrive(1, 3)
    z_arrive(-1, 3)
    u_arrive(1, 1, 3)
    u_arrive(-1, 1, 3)
    for cp in forwards:
        cp.wait_recv()

    scale2 = scale * (1.0 / LN2)
    late = 7 * R
    early_n = 12 * R

    def score_block(r0, part, count, c0, width, merge, lse_slot):
        rows = pl.ds(r0, count)
        tile = scale2 * lax.dot_general(ibuf[rows, :], tbuf[pl.ds(c0, width), :], NT, preferred_element_type=F32)
        scores[rows, pl.ds(c0, width)] = tile
        for r in range(0, count, 32):
            sub = pl.ds(r0 + r, 32)
            parts = [tile[r:r + 32, g:g + LANES] for g in range(0, width, LANES)]
            top = tree(jnp.maximum, parts)
            if merge:
                old = row_top[sub, :]
                top = jnp.maximum(top, old)
            total = tree(jnp.add, [jnp.exp2(w - top) for w in parts])
            if merge:
                total = total + row_sum[sub, :] * jnp.exp2(old - top)
            row_top[sub, :] = top
            row_sum[sub, :] = total
        if lse_slot is not None:
            lse = lse_first(row_top[rows, :].T, row_sum[rows, :].T)
            row_lse[lse_slot, :, 0:count] = jnp.broadcast_to(lse, (8, count))
        for g in range(0, width, LANES):
            parts = [tile[r:r + 8, g:g + LANES] for r in range(0, count, 8)]
            top = tree(jnp.maximum, parts)
            col_part[0, part, c0 + g:c0 + g + LANES] = top
            col_part[1, part, c0 + g:c0 + g + LANES] = tree(jnp.add, [jnp.exp2(w - top) for w in parts])

    def eight(t):
        return pl.ds(pl.multiple_of(t * 8, 8), 8)

    def early_row(t):
        return pl.multiple_of((t // 3) * (B // 2) + lax.rem(t, 3) * (late // 3), 32)

    @pl.loop(0, 6, unroll=6)
    def _(t):
        score_block(early_row(t), eight(t), late // 3, 0, early_n, False, None)

    waiting = len(forwards)
    z_arrive(1, 4)
    z_arrive(-1, 4)
    for pv in range(4):
        u_arrive(1 if pv % 2 == 0 else -1, 2, pv)

    @pl.loop(0, 6, unroll=6)
    def _(t):
        score_block(early_row(t), eight(t), late // 3, early_n, B - early_n, True, t)

    for cp in forwards[waiting:]:
        cp.wait_recv()

    @pl.loop(6, 8, unroll=2)
    def _(t):
        score_block(pl.multiple_of((t - 6) * (B // 2) + late, 32), eight(t), R, 0, B, False, t)

    me_t = u * 4 + v

    def i_row(k):
        return lax.rem(c + k // NZ, NC) * NZ + lax.rem(z + ZSTEPS[k % NZ], NZ)

    def t_row(k):
        return lax.rem(u + USTEPS[k // 4], 4) * 4 + lax.rem(v + USTEPS[k % 4], 4)

    def spread(st, mine, steps, where, ss, rs):
        return [launch(copy(st.at[mine], st.at[mine], ss.at[k], rs.at[k], where(d))) for k, d in enumerate(steps)]

    def along_z(d):
        return to(dz=d)

    st_c[c] = jnp.full((SLOTS, LANES), -1e30, F32)
    st_c[c, pl.ds(c * NZ + z, 1), R:LANES] = matched
    lse = []
    for core in range(2):
        lse += [row_lse[t, 0:1, 0:late // 3] for t in range(core * 3, core * 3 + 3)] + [row_lse[6 + core, 0:1, 0:R]]
    lse = jnp.concatenate(lse, axis=1)
    for k in range(SLOTS):
        st_c[c, pl.ds(i_row(k), 1), 0:R] = lse[:, k * R:(k + 1) * R]
    c_cp = launch(copy(st_c.at[c], st_c.at[c], sc_s.at[0], sc_r.at[0], sib))
    st_t[me_t] = jnp.zeros((SLOTS, LANES), F32)
    lse = lse_first(col_part[0], col_part[1])
    for k in range(SLOTS):
        st_t[me_t, pl.ds(t_row(k), 1), 0:R] = lse[:, k * R:(k + 1) * R]
    t_cps = spread(st_t, me_t, uv_steps, lambda d: to_uv(*d), st_s, st_r)
    c_cp.wait_recv()
    st_z[z] = lse_first(st_c[...])[0]
    z_cps = spread(st_z, z, ZSTEPS[1:], along_z, sz_s, sz_r)
    half = jnp.log2(jnp.full((1, LANES), scale * 0.5, F32))
    for cp in t_cps:
        cp.wait_recv()
    all_t[...] = lse_first(st_t[...])[0]
    for k in range(SLOTS):
        col_shift[0:1, k * R:(k + 1) * R] = (all_t[pl.ds(t_row(k), 1), :] - half)[:, 0:R]
    for cp in z_cps:
        cp.wait_recv()
    all_i[...] = lse_first(st_z[...])[0]
    for k in range(SLOTS):
        row_shift[k:k + 1, :] = all_i[pl.ds(i_row(k), 1), :] - half

    lane = lax.broadcasted_iota(jnp.int32, (1, LANES), 1)
    sum_i = jnp.sum(all_i[...], axis=0, keepdims=True) * jnp.where(lane < R, LN2, -2.0 * scale)
    sum_t = jnp.where(lane < R, LN2 * jnp.sum(all_t[...], axis=0, keepdims=True), 0.0)

    def total_of(st, n):
        return functools.reduce(jnp.add, [st[k] for k in range(n)])

    ls_x[x] = jnp.broadcast_to(sum_i, (8, LANES))
    ls_c[c] = jnp.broadcast_to(sum_t, (8, LANES))
    lx_cps = spread(ls_x, x, USTEPS[1:], lambda d: to(dx=d), lx_s, lx_r)
    lc_cps = [launch(copy(ls_c.at[c], ls_c.at[c], lc_s.at[0], lc_r.at[0], sib))]

    def make_weights(slot, c0, width, first=False):
        @pl.loop(slot, slot + 4, unroll=4)
        def _(k):
            rows = pl.ds(pl.multiple_of(k * R, R), R)
            if first:
                shift = jnp.broadcast_to(row_shift[pl.ds(k, 1), :], (LANES, LANES)).T[0:R]
                row_top[rows, :] = shift
            else:
                shift = row_top[rows, :]
            for g in range(c0, c0 + width, LANES):
                cols = pl.ds(g, LANES)
                w = scores[rows, cols]
                w = jnp.exp2(w - shift) + jnp.exp2(w - col_shift[0:1, cols])
                weights[rows, cols] = w.astype(BF16)

    def near_weights(p):
        for slot in (0, 8):
            make_weights(slot, p * TILE, TILE, p == 3)

    def p_tile(slot):
        return lax.dot_general(weights[rows_of(slot, TILE), :], tbuf[...], NN, preferred_element_type=F32)

    def sib_copy(h):
        rows = pl.ds(h * TILE, TILE)
        return copy(p_sib.at[rows], p_in.at[rows], ps_s.at[h], ps_r.at[h], sib)

    def do_sib(h):
        p_sib[pl.ds(h * TILE, TILE)] = p_tile(8 + 4 * h)
        launch(sib_copy(h))

    def p_copy(k):
        if k == 0 or k == 7:
            dz, rows = (2, 0) if k == 0 else (6, HALF)
            src = p_send.at[pl.ds(7 * R + rows, HALF)]
            return copy(src, h_recv.at[rows // HALF], pz_s.at[k], pz_r.at[k], to(dz=dz))
        src = p_send.at[rows_of(k)]
        if k in (5, 6):
            return copy(src, f_recv.at[k - 5], pz_s.at[k], pz_r.at[k], to(dz=1 if k == 5 else 7))
        return copy(src, p_recv.at[k - 1], pz_s.at[k], pz_r.at[k], to(dz=ZSTEPS[k]))

    def own_tile(h):
        tile = p_tile(4 * h)
        sib_copy(h).wait_recv()
        return tile + p_in[pl.ds(h * TILE, TILE)]

    def do_far():
        p_send[pl.ds(TILE, TILE)] = own_tile(1).astype(BF16)
        for k in (5, 6, 0, 7, 4):
            launch(p_copy(k))

    def do_near():
        tile = own_tile(0)
        p_own[...] = tile
        p_send[rows_of(1)] = tile[R:2 * R].astype(BF16)
        launch(p_copy(1))

    def do_merge():
        for k in (5, 0, 6, 7):
            p_copy(k).wait_recv()
        for i in range(2):
            @pl.loop(0, HALF // 16)
            def _(t, i=i):
                near = pl.multiple_of(t * 16, 16)
                for base, with_half in ((i * HALF, True), (HALF - i * HALF, False)):
                    rows = pl.ds(base + near, 16)
                    out = pl.ds((2 + i) * R + base + near, 16)
                    w = p_own[out] + f_recv[i, rows].astype(F32)
                    if with_half:
                        w = w + h_recv[i, pl.ds(near, 16)].astype(F32)
                    p_send[out] = w.astype(BF16)
            launch(p_copy(2 + i))

    def q_copy(p, pv):
        k = (p - 1) * 4 + pv
        return copy(q_send.at[p - 1, rows_of(pv)], q_recv.at[p - 1, rows_of(pv)], q_s.at[k], q_r.at[k], to_uv(du=USTEPS[p]))

    def do_q(p):
        tile = lax.dot_general(weights[:, rows_of(4 * p, TILE)], ibuf[...], TN, preferred_element_type=F32)
        if p:
            q_send[p - 1] = tile.astype(BF16)
            for pv in (3, 1, 2, 0):
                launch(q_copy(p, pv))
        else:
            q_own[...] = tile

    def r_copy(p):
        return copy(q_own.at[rows_of(p)], r_recv.at[p - 1], r_s.at[p - 1], r_r.at[p - 1], to_uv(dv=USTEPS[p]))

    make_weights(12, 0, B, True)
    do_sib(1)
    make_weights(4, 0, B, True)
    near_weights(3)
    do_q(3)
    for cp in lx_cps + lc_cps:
        cp.wait_recv()
    ls_y[y] = total_of(ls_x, NX)
    ls_z[z] = total_of(ls_c, NC)
    ly_cps = spread(ls_y, y, USTEPS[1:], lambda d: to(dy=d), ly_s, ly_r)
    lz_cps = spread(ls_z, z, ZSTEPS[1:], along_z, lz_s, lz_r)
    do_far()
    near_weights(1)
    do_q(1)
    near_weights(2)
    do_q(2)
    near_weights(0)
    do_sib(0)
    do_q(0)
    do_near()
    do_merge()
    for cp in ly_cps + lz_cps:
        cp.wait_recv()
    total = total_of(ls_y, NY) + total_of(ls_z, NZ)
    loss_out[0] = jnp.sum(total[0:1]) * (1.0 / (2.0 * R * NX * NY * NZ * NC))

    for pv in (3, 1, 2, 0):
        for p in range(1, 4):
            q_copy(p, pv).wait_recv()

        @pl.loop(0, R // 32)
        def _(t, pv=pv):
            rows = pl.ds(pl.multiple_of(pv * R + t * 32, 32), 32)
            q_own[rows] = functools.reduce(jnp.add, [q_recv[k, rows].astype(F32) for k in range(3)], q_own[rows])
        if pv:
            launch(r_copy(pv))
    for k in range(1, 5):
        p_copy(k).wait_recv()

    @pl.loop(0, R // 16)
    def _(t):
        rows = pl.ds(pl.multiple_of(t * 16, 16), 16)
        gi = p_own[rows] - scale * texts[rows].astype(F32)
        gi_out[rows] = functools.reduce(jnp.add, [p_recv[k, rows].astype(F32) for k in range(4)], gi)

    for p in range(1, 4):
        r_copy(p).wait_recv()

    @pl.loop(0, R // 16)
    def _(t):
        rows = pl.ds(pl.multiple_of(t * 16, 16), 16)
        gt = q_own[rows] - scale * images[rows].astype(F32)
        gt_out[rows] = functools.reduce(jnp.add, [r_recv[k, rows] for k in range(3)], gt)

    for cp in started:
        cp.wait_send()


def local(images, texts, logit_scale):
    vmem = pl.BlockSpec(memory_space=pltpu.VMEM)
    smem = pl.BlockSpec(memory_space=pltpu.SMEM)
    dma = pltpu.SemaphoreType.DMA
    scratch = [
        pltpu.VMEM((B, E), BF16), pltpu.VMEM((B, E), BF16), pltpu.VMEM((B, B), F32), pltpu.VMEM((B, B), BF16),
        pltpu.VMEM((B, LANES), F32), pltpu.VMEM((B, LANES), F32),
        pltpu.VMEM((2, 64, B), F32), pltpu.VMEM((8, B), F32),
    ]
    scratch += [pltpu.VMEM((8, 8, 2 * LANES), F32), pltpu.VMEM((SLOTS, LANES), F32)]
    scratch += [pltpu.VMEM((n, SLOTS, LANES), F32) for n in (NC, NZ)]
    scratch += [pltpu.VMEM((SLOTS, SLOTS, LANES), F32)]
    scratch += [pltpu.VMEM((SLOTS, LANES), F32)] * 2
    scratch += [pltpu.VMEM((n, 8, LANES), F32) for n in (NC, NZ, NX, NY)]
    scratch += [
        pltpu.VMEM((NZ * R, E), F32), pltpu.VMEM((NZ * R, E), F32), pltpu.VMEM((TILE, E), F32),
        pltpu.VMEM((NZ * R, E), BF16), pltpu.VMEM((4, R, E), BF16),
        pltpu.VMEM((2, R, E), BF16), pltpu.VMEM((2, HALF, E), BF16),
        pltpu.VMEM((3, TILE, E), BF16), pltpu.VMEM((3, TILE, E), BF16), pltpu.VMEM((TILE, E), F32),
        pltpu.VMEM((3, R, E), F32),
    ]
    for n in (24, 9, 15, 1, 7, 15, 1, 7, 3, 3, 2, 8, 12, 3):
        scratch += [dma((n,)), dma((n,))]
    return pl.pallas_call(
        kernel,
        out_shape=(
            jax.ShapeDtypeStruct((1,), F32),
            jax.ShapeDtypeStruct((R, E), F32),
            jax.ShapeDtypeStruct((R, E), F32),
        ),
        in_specs=[vmem, vmem, smem],
        out_specs=(smem, vmem, vmem),
        scratch_shapes=scratch,
        compiler_params=pltpu.CompilerParams(
            collective_id=0, has_side_effects=True, vmem_limit_bytes=56 * 2**20
        ),
    )(images, texts, logit_scale)


def solution(mesh):
    placed = (P(("row", "col"), None), P(("row", "col"), None), P())
    return jax.shard_map(
        local,
        mesh=mesh,
        in_specs=placed,
        out_specs=(P(), P(("row", "col"), None), P(("row", "col"), None)),
        check_vma=False,
    )
```

```python
import functools
import math

import jax
import jax.numpy as jnp
from jax import lax
from jax.experimental import pallas as pl
from jax.experimental.pallas import tpu as pltpu
from jax.sharding import PartitionSpec as P

MESH = pl.DeviceIdType.MESH
F32 = jnp.float32
BF16 = jnp.bfloat16
NT = (((1,), (1,)), ((), ()))
NN = (((1,), (0,)), ((), ()))
TN = (((0,), (0,)), ((), ()))
LN2 = math.log(2.0)
NX, NY, NZ, NC = 4, 4, 8, 2
R = 96
HALF = R // 2
PIECES = 3
PIECE = R // PIECES
E = 768
SLOTS = 16
B = SLOTS * R
LANES = 128
GROUPS = B // LANES
TILE = 4 * R
CHUNK = 256

ZSTEPS = [0, 7, 2, 6, 1, 3, 5, 4]
ZPLACE = [ZSTEPS.index(d) for d in range(NZ)]
USTEPS = [0, 1, 3, 2]
UPLACE = [USTEPS.index(d) for d in range(4)]


def tree(f, parts):
    parts = list(parts)
    while len(parts) > 1:
        parts = [f(*parts[k:k + 2]) if k + 1 < len(parts) else parts[k] for k in range(0, len(parts), 2)]
    return parts[0]


def copy(src, dst, send, recv, to):
    return pltpu.make_async_remote_copy(
        src_ref=src, dst_ref=dst, send_sem=send, recv_sem=recv, device_id=to, device_id_type=MESH
    )


def rows_of(slot, count=R):
    return pl.ds(slot * R, count)


def lse_first(top, total=None):
    high = jnp.max(top, axis=0, keepdims=True)
    part = jnp.exp2(top - high)
    part = part if total is None else part * total
    return high + jnp.log2(jnp.sum(part, axis=0, keepdims=True))


def kernel(
    images, texts, scale_ref, loss_out, gi_out, gt_out,
    ibuf, tbuf, scores, weights, row_top, row_sum, col_part, col_shift,
    row_lse, row_shift, st_c, st_z, st_t, all_i, all_t, ls_c, ls_z, ls_x, ls_y,
    p_sib, p_in, p_own, p_send, p_recv, f_recv, h_recv, q_send, q_recv, q_own, r_recv,
    zi_s, zi_r, fi_s, fi_r, ti_s, ti_r, sc_s, sc_r, sz_s, sz_r, st_s, st_r,
    lc_s, lc_r, lz_s, lz_r, lx_s, lx_r, ly_s, ly_r, ps_s, ps_r, pz_s, pz_r, q_s, q_r, r_s, r_r,
):
    row, col = lax.axis_index("row"), lax.axis_index("col")
    x, c, z, y = row // NC, lax.rem(row, NC), col // NY, lax.rem(col, NY)
    u, v = x * (1 - c) + y * c, y * (1 - c) + x * c
    scale = scale_ref[0]

    def to(dx=0, dy=0, dz=0, dc=0):
        return (lax.rem(x + dx, NX) * NC + lax.rem(c + dc, NC), lax.rem(z + dz, NZ) * NY + lax.rem(y + dy, NY))

    def to_uv(du=0, dv=0):
        return to(dx=du * (1 - c) + dv * c, dy=dv * (1 - c) + du * c)

    sib = to(dc=1)
    started = []

    def launch(cp):
        cp.start()
        started.append(cp)
        return cp

    barrier = pltpu.get_barrier_semaphore()
    uv_steps = [(du, dv) for du in USTEPS for dv in USTEPS if (du, dv) != (0, 0)]
    partners = [sib] + [to(dz=d) for d in ZSTEPS[1:]] + [to(dx=du, dy=dv) for du, dv in uv_steps]
    for d in partners:
        pl.semaphore_signal(barrier, inc=1, device_id=d, device_id_type=MESH)
    pl.semaphore_wait(barrier, len(partners))

    def z_copy(s, hop, i):
        k = (0 if s == 1 else 12) + (hop - 1) * PIECES + i
        src = pl.ds(ZPLACE[(-s * (hop - 1)) % NZ] * R + i * PIECE, PIECE)
        dst = pl.ds(ZPLACE[(-s * hop) % NZ] * R + i * PIECE, PIECE)
        held = images.at[pl.ds(i * PIECE, PIECE)] if hop == 1 else ibuf.at[src]
        return copy(held, ibuf.at[dst], zi_s.at[k], zi_r.at[k], to(dz=s % NZ))

    def last_hop(s):
        return (0, 1) if s == 1 else (2,)

    def z_arrive(s, hop):
        for i in last_hop(s) if hop == 4 else range(PIECES):
            z_copy(s, hop, i).wait_recv()
            if hop < 3 or (hop == 3 and i in last_hop(s)):
                launch(z_copy(s, hop + 1, i))
        if hop < 4:
            forward(ZPLACE[(-s * hop) % NZ] * R, R)
        else:
            forward(ZPLACE[4] * R + last_hop(s)[0] * PIECE, PIECE * len(last_hop(s)))

    forwards = []

    def forward(start, count):
        k = len(forwards)
        src = images if start == 0 else ibuf.at[pl.ds(start, count)]
        forwards.append(launch(copy(src, ibuf.at[pl.ds(B // 2 + start, count)], fi_s.at[k], fi_r.at[k], sib)))

    def v_copy(s, hop):
        k = 2 if hop == 2 else (0 if s == 1 else 1)
        dst = rows_of(UPLACE[(-s * hop) % 4])
        return copy(texts, tbuf.at[dst], ti_s.at[k], ti_r.at[k], to_uv(dv=s * hop % 4))

    def u_copy(s, hop, pv):
        src, dst = 4 * UPLACE[(-s * (hop - 1)) % 4] + pv, 4 * UPLACE[(-s * hop) % 4] + pv
        k = 3 + pv * 3 + (2 if hop == 2 else (0 if s == 1 else 1))
        held = texts if hop == 1 and pv == 0 else tbuf.at[rows_of(src)]
        return copy(held, tbuf.at[rows_of(dst)], ti_s.at[k], ti_r.at[k], to_uv(du=s % 4))

    def v_arrive(s, hop):
        v_copy(s, hop).wait_recv()
        pv = UPLACE[(-s * hop) % 4]
        launch(u_copy(1, 1, pv))
        launch(u_copy(-1, 1, pv))

    def u_arrive(s, hop, pv):
        u_copy(s, hop, pv).wait_recv()
        if hop == 1 and s == (1 if pv % 2 == 0 else -1):
            launch(u_copy(s, 2, pv))

    for i in range(PIECES):
        launch(z_copy(1, 1, i))
        launch(z_copy(-1, 1, i))
        if i == 0:
            launch(v_copy(1, 1))
            launch(v_copy(-1, 1))
    launch(v_copy(1, 2))
    launch(u_copy(1, 1, 0))
    launch(u_copy(-1, 1, 0))
    forward(0, R)
    ibuf[rows_of(0)] = images[...]
    tbuf[rows_of(0)] = texts[...]
    matched = images[...].astype(F32) * texts[...].astype(F32)
    matched = jnp.sum(matched, axis=0, keepdims=True)
    matched = tree(jnp.add, [matched[:, g:g + LANES - R] for g in range(0, E, LANES - R)])
    z_arrive(1, 1)
    z_arrive(-1, 1)
    v_arrive(1, 1)
    v_arrive(-1, 1)
    u_arrive(1, 1, 0)
    u_arrive(-1, 1, 0)
    z_arrive(1, 2)
    z_arrive(-1, 2)
    v_arrive(1, 2)
    for pv in (2, 1):
        u_arrive(1, 1, pv)
        u_arrive(-1, 1, pv)
    z_arrive(1, 3)
    z_arrive(-1, 3)
    u_arrive(1, 1, 3)
    u_arrive(-1, 1, 3)
    for cp in forwards:
        cp.wait_recv()

    scale2 = scale * (1.0 / LN2)
    late = 7 * R
    early_n = 12 * R

    def score_block(r0, part, count, c0, width, merge, lse_slot):
        rows = pl.ds(r0, count)
        tile = scale2 * lax.dot_general(ibuf[rows, :], tbuf[pl.ds(c0, width), :], NT, preferred_element_type=F32)
        scores[rows, pl.ds(c0, width)] = tile
        for r in range(0, count, 32):
            sub = pl.ds(r0 + r, 32)
            parts = [tile[r:r + 32, g:g + LANES] for g in range(0, width, LANES)]
            top = tree(jnp.maximum, parts)
            if merge:
                old = row_top[sub, :]
                top = jnp.maximum(top, old)
            total = tree(jnp.add, [jnp.exp2(w - top) for w in parts])
            if merge:
                total = total + row_sum[sub, :] * jnp.exp2(old - top)
            row_top[sub, :] = top
            row_sum[sub, :] = total
        if lse_slot is not None:
            lse = lse_first(row_top[rows, :].T, row_sum[rows, :].T)
            row_lse[lse_slot, :, 0:count] = jnp.broadcast_to(lse, (8, count))
        for g in range(0, width, LANES):
            parts = [tile[r:r + 8, g:g + LANES] for r in range(0, count, 8)]
            top = tree(jnp.maximum, parts)
            col_part[0, part, c0 + g:c0 + g + LANES] = top
            col_part[1, part, c0 + g:c0 + g + LANES] = tree(jnp.add, [jnp.exp2(w - top) for w in parts])

    def eight(t):
        return pl.ds(pl.multiple_of(t * 8, 8), 8)

    def early_row(t):
        return pl.multiple_of((t // 3) * (B // 2) + lax.rem(t, 3) * (late // 3), 32)

    @pl.loop(0, 6, unroll=6)
    def _(t):
        score_block(early_row(t), eight(t), late // 3, 0, early_n, False, None)

    waiting = len(forwards)
    z_arrive(1, 4)
    z_arrive(-1, 4)
    for pv in range(4):
        u_arrive(1 if pv % 2 == 0 else -1, 2, pv)

    @pl.loop(0, 6, unroll=6)
    def _(t):
        score_block(early_row(t), eight(t), late // 3, early_n, B - early_n, True, t)

    for cp in forwards[waiting:]:
        cp.wait_recv()

    @pl.loop(6, 8, unroll=2)
    def _(t):
        score_block(pl.multiple_of((t - 6) * (B // 2) + late, 32), eight(t), R, 0, B, False, t)

    me_t = u * 4 + v

    def i_row(k):
        return lax.rem(c + k // NZ, NC) * NZ + lax.rem(z + ZSTEPS[k % NZ], NZ)

    def t_row(k):
        return lax.rem(u + USTEPS[k // 4], 4) * 4 + lax.rem(v + USTEPS[k % 4], 4)

    def spread(st, mine, steps, where, ss, rs):
        return [launch(copy(st.at[mine], st.at[mine], ss.at[k], rs.at[k], where(d))) for k, d in enumerate(steps)]

    def along_z(d):
        return to(dz=d)

    st_c[c] = jnp.full((SLOTS, LANES), -1e30, F32)
    st_c[c, pl.ds(c * NZ + z, 1), R:LANES] = matched
    lse = []
    for core in range(2):
        lse += [row_lse[t, 0:1, 0:late // 3] for t in range(core * 3, core * 3 + 3)] + [row_lse[6 + core, 0:1, 0:R]]
    lse = jnp.concatenate(lse, axis=1)
    for k in range(SLOTS):
        st_c[c, pl.ds(i_row(k), 1), 0:R] = lse[:, k * R:(k + 1) * R]
    c_cp = launch(copy(st_c.at[c], st_c.at[c], sc_s.at[0], sc_r.at[0], sib))
    st_t[me_t] = jnp.zeros((SLOTS, LANES), F32)
    lse = lse_first(col_part[0], col_part[1])
    for k in range(SLOTS):
        st_t[me_t, pl.ds(t_row(k), 1), 0:R] = lse[:, k * R:(k + 1) * R]
    t_cps = spread(st_t, me_t, uv_steps, lambda d: to_uv(*d), st_s, st_r)
    c_cp.wait_recv()
    st_z[z] = lse_first(st_c[...])[0]
    z_cps = spread(st_z, z, ZSTEPS[1:], along_z, sz_s, sz_r)
    half = jnp.log2(jnp.full((1, LANES), scale * 0.5, F32))
    for cp in t_cps:
        cp.wait_recv()
    all_t[...] = lse_first(st_t[...])[0]
    for k in range(SLOTS):
        col_shift[0:1, k * R:(k + 1) * R] = (all_t[pl.ds(t_row(k), 1), :] - half)[:, 0:R]
    for cp in z_cps:
        cp.wait_recv()
    all_i[...] = lse_first(st_z[...])[0]
    for k in range(SLOTS):
        row_shift[k:k + 1, :] = all_i[pl.ds(i_row(k), 1), :] - half

    lane = lax.broadcasted_iota(jnp.int32, (1, LANES), 1)
    sum_i = jnp.sum(all_i[...], axis=0, keepdims=True) * jnp.where(lane < R, LN2, -2.0 * scale)
    sum_t = jnp.where(lane < R, LN2 * jnp.sum(all_t[...], axis=0, keepdims=True), 0.0)

    def total_of(st, n):
        return functools.reduce(jnp.add, [st[k] for k in range(n)])

    ls_x[x] = jnp.broadcast_to(sum_i, (8, LANES))
    ls_c[c] = jnp.broadcast_to(sum_t, (8, LANES))
    lx_cps = spread(ls_x, x, USTEPS[1:], lambda d: to(dx=d), lx_s, lx_r)
    lc_cps = [launch(copy(ls_c.at[c], ls_c.at[c], lc_s.at[0], lc_r.at[0], sib))]

    def make_weights(slot, c0, width, first=False):
        @pl.loop(slot, slot + 4, unroll=4)
        def _(k):
            rows = pl.ds(pl.multiple_of(k * R, R), R)
            if first:
                shift = jnp.broadcast_to(row_shift[pl.ds(k, 1), :], (LANES, LANES)).T[0:R]
                row_top[rows, :] = shift
            else:
                shift = row_top[rows, :]
            for g in range(c0, c0 + width, LANES):
                cols = pl.ds(g, LANES)
                w = scores[rows, cols]
                w = jnp.exp2(w - shift) + jnp.exp2(w - col_shift[0:1, cols])
                weights[rows, cols] = w.astype(BF16)

    def near_weights(p):
        for slot in (0, 8):
            make_weights(slot, p * TILE, TILE, p == 3)

    def p_tile(slot):
        return lax.dot_general(weights[rows_of(slot, TILE), :], tbuf[...], NN, preferred_element_type=F32)

    def sib_copy(h):
        rows = pl.ds(h * TILE, TILE)
        return copy(p_sib.at[rows], p_in.at[rows], ps_s.at[h], ps_r.at[h], sib)

    def do_sib(h):
        p_sib[pl.ds(h * TILE, TILE)] = p_tile(8 + 4 * h)
        launch(sib_copy(h))

    def p_copy(k):
        if k == 0 or k == 7:
            dz, rows = (2, 0) if k == 0 else (6, HALF)
            src = p_send.at[pl.ds(7 * R + rows, HALF)]
            return copy(src, h_recv.at[rows // HALF], pz_s.at[k], pz_r.at[k], to(dz=dz))
        src = p_send.at[rows_of(k)]
        if k in (5, 6):
            return copy(src, f_recv.at[k - 5], pz_s.at[k], pz_r.at[k], to(dz=1 if k == 5 else 7))
        return copy(src, p_recv.at[k - 1], pz_s.at[k], pz_r.at[k], to(dz=ZSTEPS[k]))

    def own_tile(h):
        tile = p_tile(4 * h)
        sib_copy(h).wait_recv()
        return tile + p_in[pl.ds(h * TILE, TILE)]

    def do_far():
        p_send[pl.ds(TILE, TILE)] = own_tile(1).astype(BF16)
        for k in (5, 6, 0, 7, 4):
            launch(p_copy(k))

    def do_near():
        tile = own_tile(0)
        p_own[...] = tile
        p_send[rows_of(1)] = tile[R:2 * R].astype(BF16)
        launch(p_copy(1))

    def do_merge():
        for k in (5, 0, 6, 7):
            p_copy(k).wait_recv()
        for i in range(2):
            @pl.loop(0, HALF // 16)
            def _(t, i=i):
                near = pl.multiple_of(t * 16, 16)
                for base, with_half in ((i * HALF, True), (HALF - i * HALF, False)):
                    rows = pl.ds(base + near, 16)
                    out = pl.ds((2 + i) * R + base + near, 16)
                    w = p_own[out] + f_recv[i, rows].astype(F32)
                    if with_half:
                        w = w + h_recv[i, pl.ds(near, 16)].astype(F32)
                    p_send[out] = w.astype(BF16)
            launch(p_copy(2 + i))

    def q_copy(p, pv):
        k = (p - 1) * 4 + pv
        return copy(q_send.at[p - 1, rows_of(pv)], q_recv.at[p - 1, rows_of(pv)], q_s.at[k], q_r.at[k], to_uv(du=USTEPS[p]))

    def do_q(p):
        tile = lax.dot_general(weights[:, rows_of(4 * p, TILE)], ibuf[...], TN, preferred_element_type=F32)
        if p:
            q_send[p - 1] = tile.astype(BF16)
            for pv in (3, 1, 2, 0):
                launch(q_copy(p, pv))
        else:
            q_own[...] = tile

    def r_copy(p):
        return copy(q_own.at[rows_of(p)], r_recv.at[p - 1], r_s.at[p - 1], r_r.at[p - 1], to_uv(dv=USTEPS[p]))

    make_weights(12, 0, B, True)
    do_sib(1)
    make_weights(4, 0, B, True)
    near_weights(3)
    do_q(3)
    for cp in lx_cps + lc_cps:
        cp.wait_recv()
    ls_y[y] = total_of(ls_x, NX)
    ls_z[z] = total_of(ls_c, NC)
    ly_cps = spread(ls_y, y, USTEPS[1:], lambda d: to(dy=d), ly_s, ly_r)
    lz_cps = spread(ls_z, z, ZSTEPS[1:], along_z, lz_s, lz_r)
    do_far()
    near_weights(1)
    do_q(1)
    near_weights(2)
    do_q(2)
    near_weights(0)
    do_sib(0)
    do_q(0)
    do_near()
    do_merge()
    for cp in ly_cps + lz_cps:
        cp.wait_recv()
    total = total_of(ls_y, NY) + total_of(ls_z, NZ)
    loss_out[0] = jnp.sum(total[0:1]) * (1.0 / (2.0 * R * NX * NY * NZ * NC))

    for pv in (3, 1, 2, 0):
        for p in range(1, 4):
            q_copy(p, pv).wait_recv()

        @pl.loop(0, R // 32)
        def _(t, pv=pv):
            rows = pl.ds(pl.multiple_of(pv * R + t * 32, 32), 32)
            q_own[rows] = functools.reduce(jnp.add, [q_recv[k, rows].astype(F32) for k in range(3)], q_own[rows])
        if pv:
            launch(r_copy(pv))
    for k in range(1, 5):
        p_copy(k).wait_recv()

    @pl.loop(0, R // 16)
    def _(t):
        rows = pl.ds(pl.multiple_of(t * 16, 16), 16)
        gi = p_own[rows] - scale * texts[rows].astype(F32)
        gi_out[rows] = functools.reduce(jnp.add, [p_recv[k, rows].astype(F32) for k in range(4)], gi)

    for p in range(1, 4):
        r_copy(p).wait_recv()

    @pl.loop(0, R // 16)
    def _(t):
        rows = pl.ds(pl.multiple_of(t * 16, 16), 16)
        gt = q_own[rows] - scale * images[rows].astype(F32)
        gt_out[rows] = functools.reduce(jnp.add, [r_recv[k, rows] for k in range(3)], gt)

    for cp in started:
        cp.wait_send()


def local(images, texts, logit_scale):
    vmem = pl.BlockSpec(memory_space=pltpu.VMEM)
    smem = pl.BlockSpec(memory_space=pltpu.SMEM)
    dma = pltpu.SemaphoreType.DMA
    scratch = [
        pltpu.VMEM((B, E), BF16), pltpu.VMEM((B, E), BF16), pltpu.VMEM((B, B), F32), pltpu.VMEM((B, B), BF16),
        pltpu.VMEM((B, LANES), F32), pltpu.VMEM((B, LANES), F32),
        pltpu.VMEM((2, 64, B), F32), pltpu.VMEM((8, B), F32),
    ]
    scratch += [pltpu.VMEM((8, 8, 2 * LANES), F32), pltpu.VMEM((SLOTS, LANES), F32)]
    scratch += [pltpu.VMEM((n, SLOTS, LANES), F32) for n in (NC, NZ)]
    scratch += [pltpu.VMEM((SLOTS, SLOTS, LANES), F32)]
    scratch += [pltpu.VMEM((SLOTS, LANES), F32)] * 2
    scratch += [pltpu.VMEM((n, 8, LANES), F32) for n in (NC, NZ, NX, NY)]
    scratch += [
        pltpu.VMEM((NZ * R, E), F32), pltpu.VMEM((NZ * R, E), F32), pltpu.VMEM((TILE, E), F32),
        pltpu.VMEM((NZ * R, E), BF16), pltpu.VMEM((4, R, E), BF16),
        pltpu.VMEM((2, R, E), BF16), pltpu.VMEM((2, HALF, E), BF16),
        pltpu.VMEM((3, TILE, E), BF16), pltpu.VMEM((3, TILE, E), BF16), pltpu.VMEM((TILE, E), F32),
        pltpu.VMEM((3, R, E), F32),
    ]
    for n in (24, 9, 15, 1, 7, 15, 1, 7, 3, 3, 2, 8, 12, 3):
        scratch += [dma((n,)), dma((n,))]
    return pl.pallas_call(
        kernel,
        out_shape=(
            jax.ShapeDtypeStruct((1,), F32),
            jax.ShapeDtypeStruct((R, E), F32),
            jax.ShapeDtypeStruct((R, E), F32),
        ),
        in_specs=[vmem, vmem, smem],
        out_specs=(smem, vmem, vmem),
        scratch_shapes=scratch,
        compiler_params=pltpu.CompilerParams(
            collective_id=0, has_side_effects=True, vmem_limit_bytes=44 * 2**20
        ),
    )(images, texts, logit_scale)


def solution(mesh):
    placed = (P(("row", "col"), None), P(("row", "col"), None), P())
    return jax.shard_map(
        local,
        mesh=mesh,
        in_specs=placed,
        out_specs=(P(), P(("row", "col"), None), P(("row", "col"), None)),
        check_vma=False,
    )
```

```python
import functools
import math

import jax
import jax.numpy as jnp
from jax import lax
from jax.experimental import pallas as pl
from jax.experimental.pallas import tpu as pltpu
from jax.sharding import PartitionSpec as P

MESH = pl.DeviceIdType.MESH
F32 = jnp.float32
BF16 = jnp.bfloat16
NT = (((1,), (1,)), ((), ()))
NN = (((1,), (0,)), ((), ()))
TN = (((0,), (0,)), ((), ()))
LN2 = math.log(2.0)
NX, NY, NZ, NC = 4, 4, 8, 2
R = 96
HALF = R // 2
PIECES = 3
PIECE = R // PIECES
E = 768
SLOTS = 16
B = SLOTS * R
LANES = 128
GROUPS = B // LANES
TILE = 4 * R
CHUNK = 256

ZSTEPS = [0, 7, 2, 6, 1, 3, 5, 4]
ZPLACE = [ZSTEPS.index(d) for d in range(NZ)]
USTEPS = [0, 1, 3, 2]
UPLACE = [USTEPS.index(d) for d in range(4)]


def tree(f, parts):
    parts = list(parts)
    while len(parts) > 1:
        parts = [f(*parts[k:k + 2]) if k + 1 < len(parts) else parts[k] for k in range(0, len(parts), 2)]
    return parts[0]


def copy(src, dst, send, recv, to):
    return pltpu.make_async_remote_copy(
        src_ref=src, dst_ref=dst, send_sem=send, recv_sem=recv, device_id=to, device_id_type=MESH
    )


def rows_of(slot, count=R):
    return pl.ds(slot * R, count)


def lse_first(top, total=None):
    high = jnp.max(top, axis=0, keepdims=True)
    part = jnp.exp2(top - high)
    part = part if total is None else part * total
    return high + jnp.log2(jnp.sum(part, axis=0, keepdims=True))


def kernel(
    images, texts, scale_ref, loss_out, gi_out, gt_out,
    ibuf, tbuf, scores, weights, row_top, row_sum, col_part, col_shift,
    row_lse, row_shift, st_c, st_z, st_t, all_i, all_t, ls_c, ls_z, ls_x, ls_y,
    p_sib, p_in, p_own, p_send, p_recv, f_recv, h_recv, q_send, q_recv, q_own, r_recv,
    zi_s, zi_r, fi_s, fi_r, ti_s, ti_r, sc_s, sc_r, sz_s, sz_r, st_s, st_r,
    lc_s, lc_r, lz_s, lz_r, lx_s, lx_r, ly_s, ly_r, ps_s, ps_r, pz_s, pz_r, q_s, q_r, r_s, r_r,
):
    row, col = lax.axis_index("row"), lax.axis_index("col")
    x, c, z, y = row // NC, lax.rem(row, NC), col // NY, lax.rem(col, NY)
    u, v = x * (1 - c) + y * c, y * (1 - c) + x * c
    scale = scale_ref[0]

    def to(dx=0, dy=0, dz=0, dc=0):
        return (lax.rem(x + dx, NX) * NC + lax.rem(c + dc, NC), lax.rem(z + dz, NZ) * NY + lax.rem(y + dy, NY))

    def to_uv(du=0, dv=0):
        return to(dx=du * (1 - c) + dv * c, dy=dv * (1 - c) + du * c)

    sib = to(dc=1)
    started = []

    def launch(cp):
        cp.start()
        started.append(cp)
        return cp

    barrier = pltpu.get_barrier_semaphore()
    uv_steps = [(du, dv) for du in USTEPS for dv in USTEPS if (du, dv) != (0, 0)]
    partners = [sib] + [to(dz=d) for d in ZSTEPS[1:]] + [to(dx=du, dy=dv) for du, dv in uv_steps]
    for d in partners:
        pl.semaphore_signal(barrier, inc=1, device_id=d, device_id_type=MESH)
    pl.semaphore_wait(barrier, len(partners))

    def z_copy(s, hop, i):
        k = (0 if s == 1 else 12) + (hop - 1) * PIECES + i
        src = pl.ds(ZPLACE[(-s * (hop - 1)) % NZ] * R + i * PIECE, PIECE)
        dst = pl.ds(ZPLACE[(-s * hop) % NZ] * R + i * PIECE, PIECE)
        held = images.at[pl.ds(i * PIECE, PIECE)] if hop == 1 else ibuf.at[src]
        return copy(held, ibuf.at[dst], zi_s.at[k], zi_r.at[k], to(dz=s % NZ))

    def last_hop(s):
        return (0, 1) if s == 1 else (2,)

    def z_arrive(s, hop):
        for i in last_hop(s) if hop == 4 else range(PIECES):
            z_copy(s, hop, i).wait_recv()
            if hop < 3 or (hop == 3 and i in last_hop(s)):
                launch(z_copy(s, hop + 1, i))
        if hop < 4:
            forward(ZPLACE[(-s * hop) % NZ] * R, R)
        else:
            forward(ZPLACE[4] * R + last_hop(s)[0] * PIECE, PIECE * len(last_hop(s)))

    forwards = []

    def forward(start, count):
        k = len(forwards)
        src = images if start == 0 else ibuf.at[pl.ds(start, count)]
        forwards.append(launch(copy(src, ibuf.at[pl.ds(B // 2 + start, count)], fi_s.at[k], fi_r.at[k], sib)))

    def v_copy(s, hop):
        k = 2 if hop == 2 else (0 if s == 1 else 1)
        dst = rows_of(UPLACE[(-s * hop) % 4])
        return copy(texts, tbuf.at[dst], ti_s.at[k], ti_r.at[k], to_uv(dv=s * hop % 4))

    def u_copy(s, hop, pv):
        src, dst = 4 * UPLACE[(-s * (hop - 1)) % 4] + pv, 4 * UPLACE[(-s * hop) % 4] + pv
        k = 3 + pv * 3 + (2 if hop == 2 else (0 if s == 1 else 1))
        held = texts if hop == 1 and pv == 0 else tbuf.at[rows_of(src)]
        return copy(held, tbuf.at[rows_of(dst)], ti_s.at[k], ti_r.at[k], to_uv(du=s % 4))

    def v_arrive(s, hop):
        v_copy(s, hop).wait_recv()
        pv = UPLACE[(-s * hop) % 4]
        launch(u_copy(1, 1, pv))
        launch(u_copy(-1, 1, pv))

    def u_arrive(s, hop, pv):
        u_copy(s, hop, pv).wait_recv()
        if hop == 1 and s == (1 if pv % 2 == 0 else -1):
            launch(u_copy(s, 2, pv))

    for i in range(PIECES):
        launch(z_copy(1, 1, i))
        launch(z_copy(-1, 1, i))
        if i == 0:
            launch(v_copy(1, 1))
            launch(v_copy(-1, 1))
    launch(v_copy(1, 2))
    launch(u_copy(1, 1, 0))
    launch(u_copy(-1, 1, 0))
    forward(0, R)
    ibuf[rows_of(0)] = images[...]
    tbuf[rows_of(0)] = texts[...]
    matched = images[...].astype(F32) * texts[...].astype(F32)
    matched = jnp.sum(matched, axis=0, keepdims=True)
    matched = tree(jnp.add, [matched[:, g:g + LANES - R] for g in range(0, E, LANES - R)])
    z_arrive(1, 1)
    z_arrive(-1, 1)
    v_arrive(1, 1)
    v_arrive(-1, 1)
    u_arrive(1, 1, 0)
    u_arrive(-1, 1, 0)
    z_arrive(1, 2)
    z_arrive(-1, 2)
    v_arrive(1, 2)
    for pv in (2, 1):
        u_arrive(1, 1, pv)
        u_arrive(-1, 1, pv)
    z_arrive(1, 3)
    z_arrive(-1, 3)
    u_arrive(1, 1, 3)
    u_arrive(-1, 1, 3)
    for cp in forwards:
        cp.wait_recv()

    scale2 = scale * (1.0 / LN2)
    late = 7 * R
    early_n = 12 * R

    def score_block(r0, part, count, c0, width, merge, lse_slot):
        rows = pl.ds(r0, count)
        tile = scale2 * lax.dot_general(ibuf[rows, :], tbuf[pl.ds(c0, width), :], NT, preferred_element_type=F32)
        scores[rows, pl.ds(c0, width)] = tile
        for r in range(0, count, 32):
            sub = pl.ds(r0 + r, 32)
            parts = [tile[r:r + 32, g:g + LANES] for g in range(0, width, LANES)]
            top = tree(jnp.maximum, parts)
            if merge:
                old = row_top[sub, :]
                top = jnp.maximum(top, old)
            total = tree(jnp.add, [jnp.exp2(w - top) for w in parts])
            if merge:
                total = total + row_sum[sub, :] * jnp.exp2(old - top)
            row_top[sub, :] = top
            row_sum[sub, :] = total
        if lse_slot is not None:
            lse = lse_first(row_top[rows, :].T, row_sum[rows, :].T)
            row_lse[lse_slot, :, 0:count] = jnp.broadcast_to(lse, (8, count))
        for g in range(0, width, LANES):
            parts = [tile[r:r + 8, g:g + LANES] for r in range(0, count, 8)]
            top = tree(jnp.maximum, parts)
            col_part[0, part, c0 + g:c0 + g + LANES] = top
            col_part[1, part, c0 + g:c0 + g + LANES] = tree(jnp.add, [jnp.exp2(w - top) for w in parts])

    def eight(t):
        return pl.ds(pl.multiple_of(t * 8, 8), 8)

    def early_row(t):
        return pl.multiple_of((t // 3) * (B // 2) + lax.rem(t, 3) * (late // 3), 32)

    @pl.loop(0, 6, unroll=6)
    def _(t):
        score_block(early_row(t), eight(t), late // 3, 0, early_n, False, None)

    waiting = len(forwards)
    z_arrive(1, 4)
    z_arrive(-1, 4)
    for pv in range(4):
        u_arrive(1 if pv % 2 == 0 else -1, 2, pv)

    @pl.loop(0, 6, unroll=6)
    def _(t):
        score_block(early_row(t), eight(t), late // 3, early_n, B - early_n, True, t)

    for cp in forwards[waiting:]:
        cp.wait_recv()

    @pl.loop(6, 8, unroll=2)
    def _(t):
        score_block(pl.multiple_of((t - 6) * (B // 2) + late, 32), eight(t), R, 0, B, False, t)

    me_t = u * 4 + v

    def i_row(k):
        return lax.rem(c + k // NZ, NC) * NZ + lax.rem(z + ZSTEPS[k % NZ], NZ)

    def t_row(k):
        return lax.rem(u + USTEPS[k // 4], 4) * 4 + lax.rem(v + USTEPS[k % 4], 4)

    def spread(st, mine, steps, where, ss, rs):
        return [launch(copy(st.at[mine], st.at[mine], ss.at[k], rs.at[k], where(d))) for k, d in enumerate(steps)]

    def along_z(d):
        return to(dz=d)

    st_c[c] = jnp.full((SLOTS, LANES), -1e30, F32)
    st_c[c, pl.ds(c * NZ + z, 1), R:LANES] = matched
    lse = []
    for core in range(2):
        lse += [row_lse[t, 0:1, 0:late // 3] for t in range(core * 3, core * 3 + 3)] + [row_lse[6 + core, 0:1, 0:R]]
    lse = jnp.concatenate(lse, axis=1)
    for k in range(SLOTS):
        st_c[c, pl.ds(i_row(k), 1), 0:R] = lse[:, k * R:(k + 1) * R]
    c_cp = launch(copy(st_c.at[c], st_c.at[c], sc_s.at[0], sc_r.at[0], sib))
    st_t[me_t] = jnp.zeros((SLOTS, LANES), F32)
    lse = lse_first(col_part[0], col_part[1])
    for k in range(SLOTS):
        st_t[me_t, pl.ds(t_row(k), 1), 0:R] = lse[:, k * R:(k + 1) * R]
    t_cps = spread(st_t, me_t, uv_steps, lambda d: to_uv(*d), st_s, st_r)
    c_cp.wait_recv()
    st_z[z] = lse_first(st_c[...])[0]
    z_cps = spread(st_z, z, ZSTEPS[1:], along_z, sz_s, sz_r)
    half = jnp.log2(jnp.full((1, LANES), scale * 0.5, F32))
    for cp in t_cps:
        cp.wait_recv()
    all_t[...] = lse_first(st_t[...])[0]
    for k in range(SLOTS):
        col_shift[0:1, k * R:(k + 1) * R] = (all_t[pl.ds(t_row(k), 1), :] - half)[:, 0:R]
    for cp in z_cps:
        cp.wait_recv()
    all_i[...] = lse_first(st_z[...])[0]
    for k in range(SLOTS):
        row_shift[k:k + 1, :] = all_i[pl.ds(i_row(k), 1), :] - half

    lane = lax.broadcasted_iota(jnp.int32, (1, LANES), 1)
    sum_i = jnp.sum(all_i[...], axis=0, keepdims=True) * jnp.where(lane < R, LN2, -2.0 * scale)
    sum_t = jnp.where(lane < R, LN2 * jnp.sum(all_t[...], axis=0, keepdims=True), 0.0)

    def total_of(st, n):
        return functools.reduce(jnp.add, [st[k] for k in range(n)])

    ls_x[x] = jnp.broadcast_to(sum_i, (8, LANES))
    ls_c[c] = jnp.broadcast_to(sum_t, (8, LANES))
    lx_cps = spread(ls_x, x, USTEPS[1:], lambda d: to(dx=d), lx_s, lx_r)
    lc_cps = [launch(copy(ls_c.at[c], ls_c.at[c], lc_s.at[0], lc_r.at[0], sib))]

    def make_weights(slot, c0, width, first=False):
        @pl.loop(slot, slot + 4, unroll=4)
        def _(k):
            rows = pl.ds(pl.multiple_of(k * R, R), R)
            if first:
                shift = jnp.broadcast_to(row_shift[pl.ds(k, 1), :], (LANES, LANES)).T[0:R]
                row_top[rows, :] = shift
            else:
                shift = row_top[rows, :]
            for g in range(c0, c0 + width, LANES):
                cols = pl.ds(g, LANES)
                w = scores[rows, cols]
                w = jnp.exp2(w - shift) + jnp.exp2(w - col_shift[0:1, cols])
                weights[rows, cols] = w.astype(BF16)

    def near_weights(p):
        for slot in (0, 8):
            make_weights(slot, p * TILE, TILE, p == 3)

    def p_tile(slot):
        return lax.dot_general(weights[rows_of(slot, TILE), :], tbuf[...], NN, preferred_element_type=F32)

    def sib_copy(h):
        rows = pl.ds(h * TILE, TILE)
        return copy(p_sib.at[rows], p_in.at[rows], ps_s.at[h], ps_r.at[h], sib)

    def do_sib(h):
        p_sib[pl.ds(h * TILE, TILE)] = p_tile(8 + 4 * h)
        launch(sib_copy(h))

    def p_copy(k):
        if k == 0 or k == 7:
            dz, rows = (2, 0) if k == 0 else (6, HALF)
            src = p_send.at[pl.ds(7 * R + rows, HALF)]
            return copy(src, h_recv.at[rows // HALF], pz_s.at[k], pz_r.at[k], to(dz=dz))
        src = p_send.at[rows_of(k)]
        if k in (5, 6):
            return copy(src, f_recv.at[k - 5], pz_s.at[k], pz_r.at[k], to(dz=1 if k == 5 else 7))
        return copy(src, p_recv.at[k - 1], pz_s.at[k], pz_r.at[k], to(dz=ZSTEPS[k]))

    def own_tile(h):
        tile = p_tile(4 * h)
        sib_copy(h).wait_recv()
        return tile + p_in[pl.ds(h * TILE, TILE)]

    def do_far():
        p_send[pl.ds(TILE, TILE)] = own_tile(1).astype(BF16)
        for k in (5, 6, 0, 7, 4):
            launch(p_copy(k))

    def do_near():
        tile = own_tile(0)
        p_own[...] = tile
        p_send[rows_of(1)] = tile[R:2 * R].astype(BF16)
        launch(p_copy(1))

    def do_merge():
        for k in (5, 0, 6, 7):
            p_copy(k).wait_recv()
        for i in range(2):
            @pl.loop(0, HALF // 16)
            def _(t, i=i):
                near = pl.multiple_of(t * 16, 16)
                for base, with_half in ((i * HALF, True), (HALF - i * HALF, False)):
                    rows = pl.ds(base + near, 16)
                    out = pl.ds((2 + i) * R + base + near, 16)
                    w = p_own[out] + f_recv[i, rows].astype(F32)
                    if with_half:
                        w = w + h_recv[i, pl.ds(near, 16)].astype(F32)
                    p_send[out] = w.astype(BF16)
            launch(p_copy(2 + i))

    def q_copy(p, pv):
        k = (p - 1) * 4 + pv
        return copy(q_send.at[p - 1, rows_of(pv)], q_recv.at[p - 1, rows_of(pv)], q_s.at[k], q_r.at[k], to_uv(du=USTEPS[p]))

    def do_q(p):
        tile = lax.dot_general(weights[:, rows_of(4 * p, TILE)], ibuf[...], TN, preferred_element_type=F32)
        if p:
            q_send[p - 1] = tile.astype(BF16)
            for pv in (3, 1, 2, 0):
                launch(q_copy(p, pv))
        else:
            q_own[...] = tile

    def r_copy(p):
        return copy(q_own.at[rows_of(p)], r_recv.at[p - 1], r_s.at[p - 1], r_r.at[p - 1], to_uv(dv=USTEPS[p]))

    make_weights(12, 0, B, True)
    do_sib(1)
    make_weights(4, 3 * TILE, TILE, True)
    near_weights(3)
    do_q(3)
    make_weights(4, 0, 3 * TILE)
    for cp in lx_cps + lc_cps:
        cp.wait_recv()
    ls_y[y] = total_of(ls_x, NX)
    ls_z[z] = total_of(ls_c, NC)
    ly_cps = spread(ls_y, y, USTEPS[1:], lambda d: to(dy=d), ly_s, ly_r)
    lz_cps = spread(ls_z, z, ZSTEPS[1:], along_z, lz_s, lz_r)
    do_far()
    near_weights(1)
    do_q(1)
    near_weights(2)
    do_q(2)
    near_weights(0)
    do_sib(0)
    do_q(0)
    do_near()
    do_merge()
    for cp in ly_cps + lz_cps:
        cp.wait_recv()
    total = total_of(ls_y, NY) + total_of(ls_z, NZ)
    loss_out[0] = jnp.sum(total[0:1]) * (1.0 / (2.0 * R * NX * NY * NZ * NC))

    for pv in (3, 1, 2, 0):
        for p in range(1, 4):
            q_copy(p, pv).wait_recv()

        @pl.loop(0, R // 32)
        def _(t, pv=pv):
            rows = pl.ds(pl.multiple_of(pv * R + t * 32, 32), 32)
            q_own[rows] = functools.reduce(jnp.add, [q_recv[k, rows].astype(F32) for k in range(3)], q_own[rows])
        if pv:
            launch(r_copy(pv))
    for k in range(1, 5):
        p_copy(k).wait_recv()

    @pl.loop(0, R // 16)
    def _(t):
        rows = pl.ds(pl.multiple_of(t * 16, 16), 16)
        gi = p_own[rows] - scale * texts[rows].astype(F32)
        gi_out[rows] = functools.reduce(jnp.add, [p_recv[k, rows].astype(F32) for k in range(4)], gi)

    for p in range(1, 4):
        r_copy(p).wait_recv()

    @pl.loop(0, R // 16)
    def _(t):
        rows = pl.ds(pl.multiple_of(t * 16, 16), 16)
        gt = q_own[rows] - scale * images[rows].astype(F32)
        gt_out[rows] = functools.reduce(jnp.add, [r_recv[k, rows] for k in range(3)], gt)

    for cp in started:
        cp.wait_send()


def local(images, texts, logit_scale):
    vmem = pl.BlockSpec(memory_space=pltpu.VMEM)
    smem = pl.BlockSpec(memory_space=pltpu.SMEM)
    dma = pltpu.SemaphoreType.DMA
    scratch = [
        pltpu.VMEM((B, E), BF16), pltpu.VMEM((B, E), BF16), pltpu.VMEM((B, B), F32), pltpu.VMEM((B, B), BF16),
        pltpu.VMEM((B, LANES), F32), pltpu.VMEM((B, LANES), F32),
        pltpu.VMEM((2, 64, B), F32), pltpu.VMEM((8, B), F32),
    ]
    scratch += [pltpu.VMEM((8, 8, 2 * LANES), F32), pltpu.VMEM((SLOTS, LANES), F32)]
    scratch += [pltpu.VMEM((n, SLOTS, LANES), F32) for n in (NC, NZ)]
    scratch += [pltpu.VMEM((SLOTS, SLOTS, LANES), F32)]
    scratch += [pltpu.VMEM((SLOTS, LANES), F32)] * 2
    scratch += [pltpu.VMEM((n, 8, LANES), F32) for n in (NC, NZ, NX, NY)]
    scratch += [
        pltpu.VMEM((NZ * R, E), F32), pltpu.VMEM((NZ * R, E), F32), pltpu.VMEM((TILE, E), F32),
        pltpu.VMEM((NZ * R, E), BF16), pltpu.VMEM((4, R, E), BF16),
        pltpu.VMEM((2, R, E), BF16), pltpu.VMEM((2, HALF, E), BF16),
        pltpu.VMEM((3, TILE, E), BF16), pltpu.VMEM((3, TILE, E), BF16), pltpu.VMEM((TILE, E), F32),
        pltpu.VMEM((3, R, E), F32),
    ]
    for n in (24, 9, 15, 1, 7, 15, 1, 7, 3, 3, 2, 8, 12, 3):
        scratch += [dma((n,)), dma((n,))]
    return pl.pallas_call(
        kernel,
        out_shape=(
            jax.ShapeDtypeStruct((1,), F32),
            jax.ShapeDtypeStruct((R, E), F32),
            jax.ShapeDtypeStruct((R, E), F32),
        ),
        in_specs=[vmem, vmem, smem],
        out_specs=(smem, vmem, vmem),
        scratch_shapes=scratch,
        compiler_params=pltpu.CompilerParams(
            collective_id=0, has_side_effects=True, vmem_limit_bytes=44 * 2**20
        ),
    )(images, texts, logit_scale)


def solution(mesh):
    placed = (P(("row", "col"), None), P(("row", "col"), None), P())
    return jax.shard_map(
        local,
        mesh=mesh,
        in_specs=placed,
        out_specs=(P(), P(("row", "col"), None), P(("row", "col"), None)),
        check_vma=False,
    )
```
